32 devices in a mesh: tm: 8 (over z, y), dp: 4 (over x, core).
Axes of the slice: x: 2, y: 2, z: 4, core: 2. Of those that a mesh axis runs over, the one named last changes fastest.
Arguments:
- inputs: bfloat16 [4, 8192, 1024], P('dp', 'tm'), may hold values from -6 to 6
- weights: bfloat16 [1024, 1536], replicated, may hold values from -0.1875 to 0.1875
- out_grad: bfloat16 [4, 8192, 512], P('dp', 'tm'), may hold values from -6 to 6
Outputs:
- input_grad: bfloat16 [4, 8192, 1024], P('dp', 'tm')
- weight_grad: float32 [1024, 1536], P('tm')
The draws below stay inside these ranges and needn't reach their ends.
All inputs are finite; a program needn't handle non-finite values.
Results may differ from the reference program's by a relative error of at most 0.0075.
Values sent between devices are 32-bit elements; how exact they have to be, the bound alone decides.
A program may use at most 128 MiB of HBM per device.

```python
import jax
import jax.numpy as jnp
from jax import lax

DM = 1024
H = 4
HD = 128
D = 512
CH = 256
TOKENS = 8192
REC = 4


def level_of(stream_key, dims, split, low, top_value):
    def one(dim, parts):
        draws = jax.random.uniform(jax.random.fold_in(jax.random.fold_in(stream_key, 6), dim), (parts,), jnp.float32, low / len(split), top_value / len(split))
        return jnp.repeat(jnp.exp(draws), dims[dim] // parts).reshape((-1,) + (1,) * (len(dims) - dim - 1))

    factor_of = one(*split[0])
    for cut in split[1:]:
        factor_of = factor_of * one(*cut)
    return factor_of


def normal_values(stream_key, shape, scale, most, split=(), kind=jnp.bfloat16):
    drawn = jax.random.normal(stream_key, shape, jnp.float32) * scale
    if len(split) > 0:
        drawn = level_of(stream_key, shape, split, -0.22, 0.18) * drawn
    return jnp.clip(drawn, min=-most, max=most).astype(kind)


def setup_inputs(seed: int = 0) -> dict:
    key_of = jax.random.split(jax.random.key(seed), 4)
    return {
        "inputs": normal_values(key_of[0], (REC, TOKENS, DM), 1.0, 6.0, ((0, 4), (1, 8))),
        "weights": normal_values(key_of[1], (DM, 3 * D), DM ** -0.5, 0.1875),
        "out_grad": normal_values(key_of[2], (REC, TOKENS, D), 1.0, 6.0, ((0, 4), (1, 8))),
    }


def group_grads(queries, key_rows, values, scaled_grad, state_start, grad_end):
    hi = lax.Precision.HIGHEST
    tri = (lax.broadcasted_iota(jnp.int32, (CH, CH), 0) >= lax.broadcasted_iota(jnp.int32, (CH, CH), 1)).astype(jnp.float32)
    kv_group = jnp.einsum('nshd,nshe->nhde', key_rows, values, precision=hi)
    qg_group = jnp.einsum('nthd,nthe->nhde', queries, scaled_grad, precision=hi)
    state_before = (state_start[None] + jnp.cumsum(kv_group, 0) - kv_group).astype(jnp.bfloat16).astype(jnp.float32)
    grad_after = (grad_end[None] + jnp.flip(jnp.cumsum(jnp.flip(qg_group, 0), 0), 0) - qg_group).astype(jnp.bfloat16).astype(jnp.float32)
    mix_vg = (jnp.einsum('nthe,nshe->nhts', scaled_grad, values, precision=hi) * tri).astype(jnp.bfloat16).astype(jnp.float32)
    mix_qk = (jnp.einsum('nthd,nshd->nhts', queries, key_rows, precision=hi) * tri).astype(jnp.bfloat16).astype(jnp.float32)
    grad_q = jnp.einsum('nhts,nshd->nthd', mix_vg, key_rows, precision=hi) + jnp.einsum('nthe,nhde->nthd', scaled_grad, state_before, precision=hi)
    grad_k = jnp.einsum('nhts,nthd->nshd', mix_vg, queries, precision=hi) + jnp.einsum('nshe,nhde->nshd', values, grad_after, precision=hi)
    grad_v = jnp.einsum('nhts,nthe->nshe', mix_qk, scaled_grad, precision=hi) + jnp.einsum('nshd,nhde->nshe', key_rows, grad_after, precision=hi)
    return (grad_q, grad_k, grad_v)

def reference(inputs, weights, out_grad):
    width = H * HD

    def one_recording(pair):
        record, cotangent = pair
        qkv = jnp.dot(record, weights, preferred_element_type=jnp.float32).astype(jnp.bfloat16)
        shape4 = (TOKENS // CH, CH, H, HD)
        queries = qkv[:, :width].astype(jnp.float32).reshape(shape4)
        key_rows = qkv[:, width:2 * width].astype(jnp.float32).reshape(shape4)
        values = qkv[:, 2 * width:].astype(jnp.float32).reshape(shape4)
        position = jnp.arange(TOKENS, dtype=jnp.int32).astype(jnp.float32)
        factor = 1.0 / jnp.sqrt(jnp.float32(HD) * (position + 1.0))
        scaled_grad = (cotangent.astype(jnp.float32) * factor[:, None]).astype(jnp.bfloat16).astype(jnp.float32).reshape(shape4)
        zeros = jnp.zeros((H, HD, HD), jnp.float32)
        grad_q, grad_k, grad_v = group_grads(queries, key_rows, values, scaled_grad, zeros, zeros)
        dqkv = jnp.concatenate([grad_q.reshape(TOKENS, width), grad_k.reshape(TOKENS, width), grad_v.reshape(TOKENS, width)], axis=1).astype(jnp.bfloat16)
        record_grad = lax.dot_general(dqkv, weights, (((1,), (1,)), ((), ())), preferred_element_type=jnp.float32).astype(jnp.bfloat16)
        proj_grad = lax.dot_general(record, dqkv, (((0,), (0,)), ((), ())), preferred_element_type=jnp.float32)
        return (record_grad, proj_grad)
    input_grad, proj_parts = lax.map(one_recording, (inputs, out_grad))
    return (input_grad, lax.optimization_barrier(jnp.sum(proj_parts, 0)))
```

```python
import functools

import jax
import jax.numpy as jnp
from jax import lax
from jax.experimental import pallas as pl
from jax.experimental.pallas import tpu as pltpu
from jax.sharding import PartitionSpec as P

H = 4
HD = 128
CH = 256
MESH = pl.DeviceIdType.MESH
F32 = jnp.float32
BF16 = jnp.bfloat16
NN = (((1,), (0,)), ((), ()))
NT = (((1,), (1,)), ((), ()))
TN = (((0,), (0,)), ((), ()))


def mm(a, b, dims=NN):
    return lax.dot_general(a, b, dims, preferred_element_type=F32)


def kernel(
    sizes,
    x_ref, w_ref, og_ref, dx_ref, dw_ref,
    qkv, sc, kvg, qgg, loc, dqkv, xt,
    kst, qst, kyr, qyr,
    part, crecv, a_xr, a_yr, a2, a_zr, ga, b_yr, b_zr, b2, b_xr, b3, gb,
    zk_s, zk_r, zq_s, zq_r, yk_s, yk_r, yq_s, yq_r,
    c_s, c_r, ax_s, ax_r, ay_s, ay_r, az_s, az_r, ag_s, ag_r,
    by_s, by_r, bz_s, bz_r, bx_s, bx_r, gb_s, gb_r,
):
    nz, ny, nx = sizes
    tok = x_ref.shape[0]
    nb = tok // CH
    width = H * HD
    rx = dw_ref.shape[0] // nx
    tm, dp = lax.axis_index("tm"), lax.axis_index("dp")
    z, y = tm // ny, lax.rem(tm, ny)
    x, c = dp // 2, lax.rem(dp, 2)

    def at(z_=None, y_=None, x_=None, c_=None):
        z_ = z if z_ is None else z_
        y_ = y if y_ is None else y_
        x_ = x if x_ is None else x_
        c_ = c if c_ is None else c_
        return (z_ * ny + y_, x_ * 2 + c_)

    def zpeer(d):
        return lax.rem(z + d, nz)

    def ypeer(d):
        return lax.rem(y + d, ny)

    def xpeer(d):
        return lax.rem(x + d, nx)

    def remote(src, dst, send, recv, device):
        return pltpu.make_async_remote_copy(
            src_ref=src, dst_ref=dst, send_sem=send, recv_sem=recv,
            device_id=device, device_id_type=MESH,
        )

    def head(p):
        return lax.rem(p + (H // 2) * (1 - c), H)

    peers = [at(c_=1 - c)]
    for d in range(1, nx):
        peers += [at(x_=xpeer(d)), at(x_=xpeer(d), c_=1 - c)]
    peers += [at(y_=ypeer(d)) for d in range(1, ny)]
    peers += [at(z_=zpeer(d)) for d in range(1, nz)]
    barrier = pltpu.get_barrier_semaphore()
    for peer in peers:
        pl.semaphore_signal(barrier, inc=1, device_id=peer, device_id_type=MESH)

    def project(n, carry):
        rows = pl.ds(pl.multiple_of(n * CH, CH), CH)
        r = mm(x_ref[rows, :], w_ref[...]).astype(BF16)
        pos = tm * tok + n * CH + lax.broadcasted_iota(jnp.int32, (CH, 1), 0)
        factor = 1.0 / jnp.sqrt(jnp.float32(HD) * (pos.astype(F32) + 1.0))
        g = (og_ref[rows, :].astype(F32) * factor).astype(BF16)
        for h in range(H):
            q = r[:, h * HD : (h + 1) * HD]
            k = r[:, width + h * HD : width + (h + 1) * HD]
            v = r[:, 2 * width + h * HD : 2 * width + (h + 1) * HD]
            s = g[:, h * HD : (h + 1) * HD]
            qkv[0, h, rows, :] = q
            qkv[1, h, rows, :] = k
            qkv[2, h, rows, :] = v
            sc[h, rows, :] = s
            kvg[n, h] = mm(k, v, TN)
            qgg[n, h] = mm(q, s, TN)
        return carry

    lax.fori_loop(0, nb, project, 0)

    pl.semaphore_wait(barrier, len(peers))

    @pl.when(z == 0)
    def _():
        kst[0] = jnp.zeros_like(kst[0])

    @pl.when(z == nz - 1)
    def _():
        qst[0] = jnp.zeros_like(qst[0])

    def link(p, ord_, last, nxt, st, grp, zs, zr, ys, yr_, ybuf, later):
        @pl.when(ord_ > 0)
        def _():
            remote(st.at[1, p], st.at[0, p], zs.at[p], zr.at[p], at(z_=z)).wait_recv()

        hh = head(p)
        total = st[0, p]
        for n in range(nb):
            total = total + grp[n, hh]
        st[1, p] = total

        @pl.when(ord_ < nz - 1)
        def _():
            remote(st.at[1, p], st.at[0, p], zs.at[p], zr.at[p], at(z_=nxt)).start()

        for d in range(1, ny):
            other = ypeer(d)
            which = jnp.where(later(other), 1, 0)
            remote(
                st.at[which, p], ybuf.at[d - 1, p], ys.at[d - 1, p], yr_.at[d - 1, p],
                at(y_=other),
            ).start()

    def local(n, p):
        hh = head(p)
        rows = pl.ds(pl.multiple_of(n * CH, CH), CH)
        q, k, v, s = qkv[0, hh, rows, :], qkv[1, hh, rows, :], qkv[2, hh, rows, :], sc[hh, rows, :]
        row = lax.broadcasted_iota(jnp.int32, (CH, CH), 0)
        col = lax.broadcasted_iota(jnp.int32, (CH, CH), 1)
        low, up = row >= col, row <= col
        vg = jnp.where(low, mm(s, v, NT), 0.0).astype(BF16)
        vgt = jnp.where(up, mm(v, s, NT), 0.0).astype(BF16)
        qkt = jnp.where(up, mm(k, q, NT), 0.0).astype(BF16)
        loc[0, p, rows, :] = mm(vg, k)
        loc[1, p, rows, :] = mm(vgt, q)
        loc[2, p, rows, :] = mm(qkt, s)

    steps = nz + H - 1
    items = nb * H + nb
    per = -(-items // steps)

    def step(i, carry):
        kp = i - z
        qp = i - (nz - 1 - z)

        @pl.when((kp >= 0) & (kp < H))
        def _():
            link(kp, z, nz, z + 1, kst, kvg, zk_s, zk_r, yk_s, yk_r, kyr, lambda o: o > y)

        @pl.when((qp >= 0) & (qp < H))
        def _():
            link(qp, nz - 1 - z, nz, z - 1, qst, qgg, zq_s, zq_r, yq_s, yq_r, qyr, lambda o: o < y)

        def piece(u, carry):
            idx = i * per + u

            @pl.when(idx < nb * H)
            def _():
                local(lax.rem(idx, nb), idx // nb)

            @pl.when((idx >= nb * H) & (idx < items))
            def _():
                rows = pl.ds(pl.multiple_of((idx - nb * H) * CH, CH), CH)
                xt[:, rows] = x_ref[rows, :].T

            return carry

        return lax.fori_loop(0, per, piece, carry)

    lax.fori_loop(0, steps, step, 0)

    zero = jnp.int32(0)

    def core_copy(stream, j):
        return remote(part.at[stream, j], crecv.at[stream, j], c_s.at[stream, j], c_r.at[stream, j], at(c_=1 - c))

    def ax_copy(d, j):
        o = xpeer(d)
        return remote(part.at[2, j, :, :, o], a_xr.at[d - 1, j], ax_s.at[d - 1, j], ax_r.at[d - 1, j], at(x_=o))

    def by_copy(d, j):
        o = ypeer(d)
        return remote(part.at[3, j, :, o], b_yr.at[d - 1, j], by_s.at[d - 1, j], by_r.at[d - 1, j], at(y_=o))

    def ay_copy(d, j):
        o = ypeer(d)
        return remote(part.at[2, j, :, o, x], a_yr.at[d - 1, j], ay_s.at[d - 1, j], ay_r.at[d - 1, j], at(y_=o))

    def az_copy(d, j):
        o = zpeer(d)
        return remote(a2.at[j, o], a_zr.at[d - 1, j], az_s.at[d - 1, j], az_r.at[d - 1, j], at(z_=o))

    def bz_copy(d, j):
        o = zpeer(d)
        return remote(part.at[3, j, o, y], b_zr.at[d - 1, j], bz_s.at[d - 1, j], bz_r.at[d - 1, j], at(z_=o))

    def bx_copy(d, j):
        o = xpeer(d)
        return remote(b2.at[j], b_xr.at[d - 1, j], bx_s.at[d - 1, j], bx_r.at[d - 1, j], at(x_=o))

    def gb_copy(j):
        return remote(b3.at[j], gb.at[j], gb_s.at[j], gb_r.at[j], at(c_=1 - c))

    def ag_copy(e, j):
        d, flip = e // 2, e % 2
        o = xpeer(d)
        oc = 1 - c if flip else c
        return remote(ga.at[0, j], ga.at[e, j], ag_s.at[e, j], ag_r.at[e, j], at(x_=o, c_=oc))

    def finish(p):
        hh = head(p)
        start, end = kst[0, p], qst[0, p]
        for d in range(1, ny):
            remote(kst.at[0, p], kyr.at[d - 1, p], yk_s.at[d - 1, p], yk_r.at[d - 1, p], at(y_=ypeer(d))).wait_recv()
            remote(qst.at[0, p], qyr.at[d - 1, p], yq_s.at[d - 1, p], yq_r.at[d - 1, p], at(y_=ypeer(d))).wait_recv()
            start = start + kyr[d - 1, p]
            end = end + qyr[d - 1, p]
        cols = [pl.ds(pl.multiple_of(j * width + hh * HD, HD), HD) for j in range(3)]
        for n in range(nb):
            rows = pl.ds(n * CH, CH)
            dq = loc[0, p, rows, :] + mm(sc[hh, rows, :], start.astype(BF16), NT)
            dqkv[rows, cols[0]] = dq.astype(BF16)
            start = start + kvg[n, hh]
        for n in range(nb - 1, -1, -1):
            rows = pl.ds(n * CH, CH)
            after = end.astype(BF16)
            dk = loc[1, p, rows, :] + mm(qkv[2, hh, rows, :], after, NT)
            dv = loc[2, p, rows, :] + mm(qkv[1, hh, rows, :], after)
            dqkv[rows, cols[1]] = dk.astype(BF16)
            dqkv[rows, cols[2]] = dv.astype(BF16)
            end = end + qgg[n, hh]
        d = jnp.concatenate([dqkv[:, cols[j]] for j in range(3)], axis=1)
        dm = xt.shape[0]
        m = 256
        zrows = dm // nz

        def slab(i, carry):
            rows = pl.ds(pl.multiple_of(i * zrows, zrows), zrows)
            r = mm(xt[rows, :], d)
            for j in range(3):
                part[p, j, i] = r[:, j * HD : (j + 1) * HD].reshape(ny, nx, rx, HD)
            return carry

        lax.fori_loop(0, nz, slab, 0)

    def head_step(p, carry):
        finish(p)

        @pl.when(p < 2)
        def _():
            for j in range(3):
                core_copy(p, j).start()

        @pl.when(p >= 2)
        def _():
            for j in range(3):
                core_copy(p - 2, j).wait_recv()
                for i in range(nz):
                    part[p, j, i] = part[p, j, i] + crecv[p - 2, j, i]

                @pl.when(p == 2)
                def _():
                    for d in range(1, nx):
                        ax_copy(d, j).start()

                @pl.when(p == 3)
                def _():
                    for d in range(1, ny):
                        by_copy(d, j).start()

        return carry

    lax.fori_loop(0, H, head_step, 0)

    def input_rows(i, carry):
        rows = pl.ds(pl.multiple_of(i * CH, CH), CH)
        dx_ref[rows, :] = mm(dqkv[rows, :], w_ref[...], NT).astype(BF16)
        return carry

    lax.fori_loop(0, nb, input_rows, 0)

    def stage1(j, carry):
        for d in range(1, nx):
            ax_copy(d, j).wait_recv()
        for i in range(nz):
            t = part[2, j, i, :, x]
            for d in range(1, nx):
                t = t + a_xr[d - 1, j, i]
            part[2, j, i, :, x] = t
        for d in range(1, ny):
            ay_copy(d, j).start()
        for d in range(1, ny):
            by_copy(d, j).wait_recv()
        for i in range(nz):
            t = part[3, j, i, y]
            for d in range(1, ny):
                t = t + b_yr[d - 1, j, i]
            part[3, j, i, y] = t
        for d in range(1, nz):
            bz_copy(d, j).start()
        return carry

    def stage2(j, carry):
        for d in range(1, ny):
            ay_copy(d, j).wait_recv()
        for i in range(nz):
            t = part[2, j, i, y, x]
            for d in range(1, ny):
                t = t + a_yr[d - 1, j, i]
            a2[j, i] = t
        for d in range(1, nz):
            az_copy(d, j).start()
        for d in range(1, nz):
            bz_copy(d, j).wait_recv()
        t = part[3, j, z, y]
        for d in range(1, nz):
            t = t + b_zr[d - 1, j]
        b2[j] = t
        for d in range(1, nx):
            bx_copy(d, j).start()
        return carry

    def stage3(j, carry):
        for d in range(1, nz):
            az_copy(d, j).wait_recv()
        t = a2[j, z]
        for d in range(1, nz):
            t = t + a_zr[d - 1, j]
        ga[0, j] = t
        for e in range(1, 2 * nx):
            ag_copy(e, j).start()
        for d in range(1, nx):
            bx_copy(d, j).wait_recv()
        t = b2[j]
        for d in range(1, nx):
            t = t + b_xr[d - 1, j]
        b3[j] = t
        gb_copy(j).start()
        cols = pl.ds(pl.multiple_of(j * width + (2 * c + 1) * HD, HD), HD)
        dw_ref[:, cols] = t.reshape(nx * rx, HD)
        return carry

    def stage4(j, carry):
        for e in range(2 * nx):
            if e:
                ag_copy(e, j).wait_recv()
            d, flip = e // 2, e % 2
            o = lax.rem(x - d + nx, nx)
            oc = 1 - c if flip else c
            rows = pl.ds(pl.multiple_of(o * rx, rx), rx)
            cols = pl.ds(pl.multiple_of(j * width + 2 * oc * HD, HD), HD)
            dw_ref[rows, cols] = ga[e, j]
        gb_copy(j).wait_recv()
        cols = pl.ds(pl.multiple_of(j * width + (2 * (1 - c) + 1) * HD, HD), HD)
        dw_ref[:, cols] = gb[j].reshape(nx * rx, HD)
        return carry

    lax.fori_loop(0, 3, stage1, 0)
    lax.fori_loop(0, 3, stage2, 0)
    lax.fori_loop(0, 3, stage3, 0)
    lax.fori_loop(0, 3, stage4, 0)

    def drain_state(p, carry):
        @pl.when(z < nz - 1)
        def _():
            remote(kst.at[1, p], kst.at[0, p], zk_s.at[p], zk_r.at[p], at(z_=z)).wait_send()

        @pl.when(z > 0)
        def _():
            remote(qst.at[1, p], qst.at[0, p], zq_s.at[p], zq_r.at[p], at(z_=z)).wait_send()

        for d in range(1, ny):
            remote(kst.at[0, p], kyr.at[d - 1, p], yk_s.at[d - 1, p], yk_r.at[d - 1, p], at(y_=ypeer(d))).wait_send()
            remote(qst.at[0, p], qyr.at[d - 1, p], yq_s.at[d - 1, p], yq_r.at[d - 1, p], at(y_=ypeer(d))).wait_send()
        return carry

    def drain(j, carry):
        core_copy(0, j).wait_send()
        core_copy(1, j).wait_send()
        for d in range(1, nx):
            ax_copy(d, j).wait_send()
            bx_copy(d, j).wait_send()
        for d in range(1, ny):
            ay_copy(d, j).wait_send()
            by_copy(d, j).wait_send()
        for d in range(1, nz):
            az_copy(d, j).wait_send()
            bz_copy(d, j).wait_send()
        for e in range(1, 2 * nx):
            ag_copy(e, j).wait_send()
        gb_copy(j).wait_send()
        return carry

    lax.fori_loop(0, H, drain_state, 0)
    lax.fori_loop(0, 3, drain, 0)


def shards(nz, ny, nx, inputs, weights, out_grad):
    record, cot = inputs[0], out_grad[0]
    tok, dm = record.shape
    nb = tok // CH
    rx = dm // (nz * ny * nx)
    V = pltpu.VMEM
    D = pltpu.SemaphoreType.DMA
    scratch = [
        V((3, H, tok, HD), BF16), V((H, tok, HD), BF16),
        V((nb, H, HD, HD), F32), V((nb, H, HD, HD), F32),
        V((3, H, tok, HD), F32), V((tok, 3 * H * HD), BF16), V((dm, tok), BF16),
        V((2, H, HD, HD), F32), V((2, H, HD, HD), F32),
        V((ny - 1, H, HD, HD), F32), V((ny - 1, H, HD, HD), F32),
        V((4, 3, nz, ny, nx, rx, HD), F32), V((2, 3, nz, ny, nx, rx, HD), F32),
        V((nx - 1, 3, nz, ny, rx, HD), F32), V((ny - 1, 3, nz, rx, HD), F32),
        V((3, nz, rx, HD), F32), V((nz - 1, 3, rx, HD), F32), V((2 * nx, 3, rx, HD), F32),
        V((ny - 1, 3, nz, nx, rx, HD), F32), V((nz - 1, 3, nx, rx, HD), F32),
        V((3, nx, rx, HD), F32), V((nx - 1, 3, nx, rx, HD), F32),
        V((3, nx, rx, HD), F32), V((3, nx, rx, HD), F32),
        D((H,)), D((H,)), D((H,)), D((H,)),
        D((ny - 1, H)), D((ny - 1, H)), D((ny - 1, H)), D((ny - 1, H)),
        D((2, 3)), D((2, 3)), D((nx - 1, 3)), D((nx - 1, 3)), D((ny - 1, 3)), D((ny - 1, 3)),
        D((nz - 1, 3)), D((nz - 1, 3)), D((2 * nx, 3)), D((2 * nx, 3)),
        D((ny - 1, 3)), D((ny - 1, 3)), D((nz - 1, 3)), D((nz - 1, 3)),
        D((nx - 1, 3)), D((nx - 1, 3)), D((3,)), D((3,)),
    ]
    vm = pl.BlockSpec(memory_space=pltpu.VMEM)
    dx, dw = pl.pallas_call(
        functools.partial(kernel, (nz, ny, nx)),
        out_shape=(
            jax.ShapeDtypeStruct((tok, dm), BF16),
            jax.ShapeDtypeStruct((dm // (nz * ny), weights.shape[1]), F32),
        ),
        in_specs=[vm, vm, vm],
        out_specs=(vm, vm),
        scratch_shapes=scratch,
        compiler_params=pltpu.CompilerParams(
            collective_id=0, has_side_effects=True, vmem_limit_bytes=60 * 1024 * 1024
        ),
    )(record, weights, cot)
    return dx[None], dw


def solution(mesh):
    nx = mesh.shape["dp"] // 2
    ny = nx if mesh.shape["tm"] % nx == 0 else 1
    nz = mesh.shape["tm"] // ny
    return jax.shard_map(
        functools.partial(shards, nz, ny, nx),
        mesh=mesh,
        in_specs=(P("dp", "tm", None), P(), P("dp", "tm", None)),
        out_specs=(P("dp", "tm", None), P("tm", None)),
        check_vma=False,
    )
```

```python
import functools

import jax
import jax.numpy as jnp
from jax import lax
from jax.experimental import pallas as pl
from jax.experimental.pallas import tpu as pltpu
from jax.sharding import PartitionSpec as P

H = 4
HD = 128
CH = 256
MESH = pl.DeviceIdType.MESH
F32 = jnp.float32
BF16 = jnp.bfloat16
NN = (((1,), (0,)), ((), ()))
NT = (((1,), (1,)), ((), ()))
TN = (((0,), (0,)), ((), ()))


def mm(a, b, dims=NN):
    return lax.dot_general(a, b, dims, preferred_element_type=F32)


FIRST = ((0, 0), (0, 1), (0, 2), (1, 0))
SECOND = ((1, 1), (1, 2))


def kernel(
    sizes,
    x_ref, w_ref, og_ref, dx_ref, dw_ref,
    qkv, sc, kvg, qgg, loc, dqkv, xt, dxs, dx_sem,
    kst, qst, kyr, qyr,
    part, crecv, a_xr, a_yr, a2, a_zr, ga, b_yr, b_zr, b2, b_xr, b3, gb,
    zk_s, zk_r, zq_s, zq_r, yk_s, yk_r, yq_s, yq_r,
    c_s, c_r, ax_s, ax_r, ay_s, ay_r, az_s, az_r, ag_s, ag_r,
    by_s, by_r, bz_s, bz_r, bx_s, bx_r, gb_s, gb_r,
):
    nz, ny, nx = sizes
    tok = x_ref.shape[0]
    nb = tok // CH
    width = H * HD
    rx = dw_ref.shape[0] // nx
    dm = x_ref.shape[1]
    tm, dp = lax.axis_index("tm"), lax.axis_index("dp")
    z, y = tm // ny, lax.rem(tm, ny)
    x, c = dp // 2, lax.rem(dp, 2)

    def at(z_=None, y_=None, x_=None, c_=None):
        z_ = z if z_ is None else z_
        y_ = y if y_ is None else y_
        x_ = x if x_ is None else x_
        c_ = c if c_ is None else c_
        return (z_ * ny + y_, x_ * 2 + c_)

    def zpeer(d):
        return lax.rem(z + d, nz)

    def ypeer(d):
        return lax.rem(y + d, ny)

    def xpeer(d):
        return lax.rem(x + d, nx)

    def remote(src, dst, send, recv, device):
        return pltpu.make_async_remote_copy(
            src_ref=src, dst_ref=dst, send_sem=send, recv_sem=recv,
            device_id=device, device_id_type=MESH,
        )

    def head(p):
        return 2 * lax.rem(p + 1 - c, 2) + p // 2

    peers = [at(c_=1 - c)]
    for d in range(1, nx):
        peers += [at(x_=xpeer(d)), at(x_=xpeer(d), c_=1 - c)]
    peers += [at(y_=ypeer(d)) for d in range(1, ny)]
    peers += [at(z_=zpeer(d)) for d in range(1, nz)]
    barrier = pltpu.get_barrier_semaphore()
    for peer in peers:
        pl.semaphore_signal(barrier, inc=1, device_id=peer, device_id_type=MESH)

    def project(n, carry):
        rows = pl.ds(pl.multiple_of(n * CH, CH), CH)
        r = mm(x_ref[rows, :], w_ref[...]).astype(BF16)
        pos = tm * tok + n * CH + lax.broadcasted_iota(jnp.int32, (CH, 1), 0)
        factor = 1.0 / jnp.sqrt(jnp.float32(HD) * (pos.astype(F32) + 1.0))
        g = (og_ref[rows, :].astype(F32) * factor).astype(BF16)
        for h in range(H):
            q = r[:, h * HD : (h + 1) * HD]
            k = r[:, width + h * HD : width + (h + 1) * HD]
            v = r[:, 2 * width + h * HD : 2 * width + (h + 1) * HD]
            s = g[:, h * HD : (h + 1) * HD]
            qkv[0, h, rows, :] = q
            qkv[1, h, rows, :] = k
            qkv[2, h, rows, :] = v
            sc[h, rows, :] = s
            kvg[n, h] = mm(k, v, TN)
            qgg[n, h] = mm(q, s, TN)
        return carry

    lax.fori_loop(0, nb, project, 0)

    pl.semaphore_wait(barrier, len(peers))

    @pl.when(z == 0)
    def _():
        kst[0] = jnp.zeros_like(kst[0])

    @pl.when(z == nz - 1)
    def _():
        qst[0] = jnp.zeros_like(qst[0])

    def link(p, ord_, last, nxt, st, grp, zs, zr, ys, yr_, ybuf, later):
        @pl.when(ord_ > 0)
        def _():
            remote(st.at[1, p], st.at[0, p], zs.at[p], zr.at[p], at(z_=z)).wait_recv()

        hh = head(p)
        total = st[0, p]
        for n in range(nb):
            total = total + grp[n, hh]
        st[1, p] = total

        @pl.when(ord_ < nz - 1)
        def _():
            remote(st.at[1, p], st.at[0, p], zs.at[p], zr.at[p], at(z_=nxt)).start()

        for d in range(1, ny):
            other = ypeer(d)
            which = jnp.where(later(other), 1, 0)
            remote(
                st.at[which, p], ybuf.at[d - 1, p], ys.at[d - 1, p], yr_.at[d - 1, p],
                at(y_=other),
            ).start()

    def local(n, p):
        hh = head(p)
        rows = pl.ds(pl.multiple_of(n * CH, CH), CH)
        q, k, v, s = qkv[0, hh, rows, :], qkv[1, hh, rows, :], qkv[2, hh, rows, :], sc[hh, rows, :]
        row = lax.broadcasted_iota(jnp.int32, (CH, CH), 0)
        col = lax.broadcasted_iota(jnp.int32, (CH, CH), 1)
        low, up = row >= col, row <= col
        vg = jnp.where(low, mm(s, v, NT), 0.0).astype(BF16)
        vgt = jnp.where(up, mm(v, s, NT), 0.0).astype(BF16)
        qkt = jnp.where(up, mm(k, q, NT), 0.0).astype(BF16)
        loc[0, p, rows, :] = mm(vg, k)
        loc[1, p, rows, :] = mm(vgt, q)
        loc[2, p, rows, :] = mm(qkt, s)

    def core_copy(slot, j):
        return remote(part.at[2 * slot, j], crecv.at[slot, j], c_s.at[slot, j], c_r.at[slot, j], at(c_=1 - c))

    def mine(g):
        return part.at[2 * g[0] + 1, g[1]]

    def ax_copy(d, a):
        o = xpeer(d)
        return remote(
            mine(FIRST[a]).at[:, :, o], a_xr.at[d - 1, a], ax_s.at[d - 1, a], ax_r.at[d - 1, a], at(x_=o)
        )

    def ay_copy(d, a):
        o = ypeer(d)
        return remote(
            mine(FIRST[a]).at[:, o, x], a_yr.at[d - 1, a], ay_s.at[d - 1, a], ay_r.at[d - 1, a], at(y_=o)
        )

    def az_copy(d, a):
        o = zpeer(d)
        return remote(a2.at[a, o], a_zr.at[d - 1, a], az_s.at[d - 1, a], az_r.at[d - 1, a], at(z_=o))

    def by_copy(d, b):
        o = ypeer(d)
        return remote(
            mine(SECOND[b]).at[:, o], b_yr.at[d - 1, b], by_s.at[d - 1, b], by_r.at[d - 1, b], at(y_=o)
        )

    def bz_copy(d, b):
        o = zpeer(d)
        return remote(
            mine(SECOND[b]).at[o, y], b_zr.at[d - 1, b], bz_s.at[d - 1, b], bz_r.at[d - 1, b], at(z_=o)
        )

    def bx_copy(d, b):
        o = xpeer(d)
        return remote(b2.at[b], b_xr.at[d - 1, b], bx_s.at[d - 1, b], bx_r.at[d - 1, b], at(x_=o))

    def gb_copy(b):
        return remote(b3.at[b], gb.at[b], gb_s.at[b], gb_r.at[b], at(c_=1 - c))

    def ag_copy(e, j):
        d, flip = e // 2, e % 2
        o = xpeer(d)
        oc = 1 - c if flip else c
        return remote(ga.at[0, j], ga.at[e, j], ag_s.at[e, j], ag_r.at[e, j], at(x_=o, c_=oc))

    def finish(p):
        hh = head(p)
        start, end = kst[0, p], qst[0, p]
        for d in range(1, ny):
            remote(kst.at[0, p], kyr.at[d - 1, p], yk_s.at[d - 1, p], yk_r.at[d - 1, p], at(y_=ypeer(d))).wait_recv()
            remote(qst.at[0, p], qyr.at[d - 1, p], yq_s.at[d - 1, p], yq_r.at[d - 1, p], at(y_=ypeer(d))).wait_recv()
            start = start + kyr[d - 1, p]
            end = end + qyr[d - 1, p]
        cols = [pl.ds(pl.multiple_of(j * width + hh * HD, HD), HD) for j in range(3)]
        for n in range(nb):
            rows = pl.ds(n * CH, CH)
            dq = loc[0, p, rows, :] + mm(sc[hh, rows, :], start.astype(BF16), NT)
            dqkv[rows, cols[0]] = dq.astype(BF16)
            start = start + kvg[n, hh]
        for n in range(nb - 1, -1, -1):
            rows = pl.ds(n * CH, CH)
            after = end.astype(BF16)
            dk = loc[1, p, rows, :] + mm(qkv[2, hh, rows, :], after, NT)
            dv = loc[2, p, rows, :] + mm(qkv[1, hh, rows, :], after)
            dqkv[rows, cols[1]] = dk.astype(BF16)
            dqkv[rows, cols[2]] = dv.astype(BF16)
            end = end + qgg[n, hh]
        d = jnp.concatenate([dqkv[:, cols[j]] for j in range(3)], axis=1)
        zrows = dm // nz

        def slab(i, carry):
            rows = pl.ds(pl.multiple_of(i * zrows, zrows), zrows)
            r = mm(xt[rows, :], d)
            for j in range(3):
                part[p, j, i] = r[:, j * HD : (j + 1) * HD].reshape(ny, nx, rx, HD)
            return carry

        lax.fori_loop(0, nz, slab, 0)

    def head_step(p):
        finish(p)
        slot = p // 2

        @pl.when(lax.rem(p, 2) == 0)
        def _():
            for j in range(3):
                core_copy(slot, j).start()

        @pl.when(lax.rem(p, 2) == 1)
        def _():
            for j in range(3):
                core_copy(slot, j).wait_recv()
                for i in range(nz):
                    part[p, j, i] = part[p, j, i] + crecv[slot, j, i]
                for s_ in range(2):

                    @pl.when(slot == s_)
                    def _():
                        if (s_, j) in FIRST:
                            for d in range(1, nx):
                                ax_copy(d, FIRST.index((s_, j))).start()
                        else:
                            for d in range(1, ny):
                                by_copy(d, SECOND.index((s_, j))).start()

    items = nb * (H + 1)
    per = 1
    while any((nz + p + 1) * per < nb * (p + 2) for p in range(H)):
        per += 1

    def step(i, carry):
        kp = i - z
        qp = i - (nz - 1 - z)

        @pl.when((kp >= 0) & (kp < H))
        def _():
            link(kp, z, nz, z + 1, kst, kvg, zk_s, zk_r, yk_s, yk_r, kyr, lambda o: o > y)

        @pl.when((qp >= 0) & (qp < H))
        def _():
            link(qp, nz - 1 - z, nz, z - 1, qst, qgg, zq_s, zq_r, yq_s, yq_r, qyr, lambda o: o < y)

        def piece(u, carry):
            idx = i * per + u
            group, n = idx // nb, lax.rem(idx, nb)

            @pl.when((idx < items) & (group != 1))
            def _():
                local(n, jnp.where(group == 0, 0, group - 1))

            @pl.when(group == 1)
            def _():
                rows = pl.ds(pl.multiple_of(n * CH, CH), CH)
                xt[:, rows] = x_ref[rows, :].T

            return carry

        lax.fori_loop(0, per, piece, 0)

        @pl.when(i >= nz)
        def _():
            head_step(i - nz)

        return carry

    lax.fori_loop(0, nz + H, step, 0)

    def out_copy(i):
        rows = pl.ds(i * CH, CH)
        return pltpu.make_async_copy(dxs.at[rows, :], dx_ref.at[rows, :], dx_sem.at[i])

    def rows_of(i):
        rows = pl.ds(i * CH, CH)
        dxs[rows, :] = mm(dqkv[rows, :], w_ref[...], NT)
        out_copy(i).start()

    def a_one(a):
        for d in range(1, nx):
            ax_copy(d, a).wait_recv()
        own = mine(FIRST[a])
        for i in range(nz):
            t = own[i, :, x]
            for d in range(1, nx):
                t = t + a_xr[d - 1, a, i]
            own[i, :, x] = t
        for d in range(1, ny):
            ay_copy(d, a).start()

    def a_two(a):
        for d in range(1, ny):
            ay_copy(d, a).wait_recv()
        own = mine(FIRST[a])
        for i in range(nz):
            t = own[i, y, x]
            for d in range(1, ny):
                t = t + a_yr[d - 1, a, i]
            a2[a, i] = t
        for d in range(1, nz):
            az_copy(d, a).start()

    def a_three(a):
        for d in range(1, nz):
            az_copy(d, a).wait_recv()
        t = a2[a, z]
        for d in range(1, nz):
            t = t + a_zr[d - 1, a]
        ga[0, a] = t
        for e in range(1, 2 * nx):
            ag_copy(e, a).start()

    def cols_of(g, core):
        return pl.ds(pl.multiple_of(g[1] * width + (2 * core + g[0]) * HD, HD), HD)

    def a_last(a):
        for e in range(2 * nx):
            if e:
                ag_copy(e, a).wait_recv()
            d, flip = e // 2, e % 2
            o = lax.rem(x - d + nx, nx)
            rows = pl.ds(pl.multiple_of(o * rx, rx), rx)
            dw_ref[rows, cols_of(FIRST[a], 1 - c if flip else c)] = ga[e, a]

    def b_one(b):
        for d in range(1, ny):
            by_copy(d, b).wait_recv()
        own = mine(SECOND[b])
        for i in range(nz):
            t = own[i, y]
            for d in range(1, ny):
                t = t + b_yr[d - 1, b, i]
            own[i, y] = t
        for d in range(1, nz):
            bz_copy(d, b).start()

    def b_two(b):
        for d in range(1, nz):
            bz_copy(d, b).wait_recv()
        t = mine(SECOND[b])[z, y]
        for d in range(1, nz):
            t = t + b_zr[d - 1, b]
        b2[b] = t
        for d in range(1, nx):
            bx_copy(d, b).start()

    def b_three(b):
        for d in range(1, nx):
            bx_copy(d, b).wait_recv()
        t = b2[b]
        for d in range(1, nx):
            t = t + b_xr[d - 1, b]
        b3[b] = t
        gb_copy(b).start()
        dw_ref[:, cols_of(SECOND[b], c)] = t.reshape(nx * rx, HD)

    def b_last(b):
        gb_copy(b).wait_recv()
        dw_ref[:, cols_of(SECOND[b], 1 - c)] = gb[b].reshape(nx * rx, HD)

    order = [
        (a_one, 0), (rows_of, 0), (b_one, 0), (rows_of, 1), (a_one, 1), (rows_of, 2), (a_two, 0),
        (rows_of, 3), (b_one, 1), (b_two, 0), (a_one, 2), (a_two, 1), (a_three, 0), (b_three, 0),
        (a_one, 3), (a_two, 2), (b_two, 1), (a_three, 1), (b_three, 1), (a_two, 3), (a_three, 2),
        (a_three, 3), (b_last, 0), (b_last, 1), (a_last, 0), (a_last, 1), (a_last, 2), (a_last, 3),
    ]
    for work, i in order:
        work(i)
    for i in range(nb):
        out_copy(i).wait()

    def drain_state(p, carry):
        @pl.when(z < nz - 1)
        def _():
            remote(kst.at[1, p], kst.at[0, p], zk_s.at[p], zk_r.at[p], at(z_=z)).wait_send()

        @pl.when(z > 0)
        def _():
            remote(qst.at[1, p], qst.at[0, p], zq_s.at[p], zq_r.at[p], at(z_=z)).wait_send()

        for d in range(1, ny):
            remote(kst.at[0, p], kyr.at[d - 1, p], yk_s.at[d - 1, p], yk_r.at[d - 1, p], at(y_=ypeer(d))).wait_send()
            remote(qst.at[0, p], qyr.at[d - 1, p], yq_s.at[d - 1, p], yq_r.at[d - 1, p], at(y_=ypeer(d))).wait_send()
        return carry

    lax.fori_loop(0, H, drain_state, 0)
    for j in range(3):
        core_copy(0, j).wait_send()
        core_copy(1, j).wait_send()
    for a in range(len(FIRST)):
        for d in range(1, nx):
            ax_copy(d, a).wait_send()
        for d in range(1, ny):
            ay_copy(d, a).wait_send()
        for d in range(1, nz):
            az_copy(d, a).wait_send()
        for e in range(1, 2 * nx):
            ag_copy(e, a).wait_send()
    for b in range(len(SECOND)):
        for d in range(1, ny):
            by_copy(d, b).wait_send()
        for d in range(1, nz):
            bz_copy(d, b).wait_send()
        for d in range(1, nx):
            bx_copy(d, b).wait_send()
        gb_copy(b).wait_send()


def shards(nz, ny, nx, inputs, weights, out_grad):
    record, cot = inputs[0], out_grad[0]
    tok, dm = record.shape
    nb = tok // CH
    rx = dm // (nz * ny * nx)
    na, ns = len(FIRST), len(SECOND)
    V = pltpu.VMEM
    D = pltpu.SemaphoreType.DMA
    scratch = [
        V((3, H, tok, HD), BF16), V((H, tok, HD), BF16),
        V((nb, H, HD, HD), F32), V((nb, H, HD, HD), F32),
        V((3, H, tok, HD), F32), V((tok, 3 * H * HD), BF16), V((dm, tok), BF16),
        V((tok, dm), F32), D((nb,)),
        V((2, H, HD, HD), F32), V((2, H, HD, HD), F32),
        V((ny - 1, H, HD, HD), F32), V((ny - 1, H, HD, HD), F32),
        V((4, 3, nz, ny, nx, rx, HD), F32), V((2, 3, nz, ny, nx, rx, HD), F32),
        V((nx - 1, na, nz, ny, rx, HD), F32), V((ny - 1, na, nz, rx, HD), F32),
        V((na, nz, rx, HD), F32), V((nz - 1, na, rx, HD), F32), V((2 * nx, na, rx, HD), F32),
        V((ny - 1, ns, nz, nx, rx, HD), F32), V((nz - 1, ns, nx, rx, HD), F32),
        V((ns, nx, rx, HD), F32), V((nx - 1, ns, nx, rx, HD), F32),
        V((ns, nx, rx, HD), F32), V((ns, nx, rx, HD), F32),
        D((H,)), D((H,)), D((H,)), D((H,)),
        D((ny - 1, H)), D((ny - 1, H)), D((ny - 1, H)), D((ny - 1, H)),
        D((2, 3)), D((2, 3)), D((nx - 1, na)), D((nx - 1, na)), D((ny - 1, na)), D((ny - 1, na)),
        D((nz - 1, na)), D((nz - 1, na)), D((2 * nx, na)), D((2 * nx, na)),
        D((ny - 1, ns)), D((ny - 1, ns)), D((nz - 1, ns)), D((nz - 1, ns)),
        D((nx - 1, ns)), D((nx - 1, ns)), D((ns,)), D((ns,)),
    ]
    vm = pl.BlockSpec(memory_space=pltpu.VMEM)
    dx, dw = pl.pallas_call(
        functools.partial(kernel, (nz, ny, nx)),
        out_shape=(
            jax.ShapeDtypeStruct((tok, dm), F32),
            jax.ShapeDtypeStruct((dm // (nz * ny), weights.shape[1]), F32),
        ),
        in_specs=[vm, vm, vm],
        out_specs=(pl.BlockSpec(memory_space=pl.ANY), vm),
        scratch_shapes=scratch,
        compiler_params=pltpu.CompilerParams(
            collective_id=0, has_side_effects=True, vmem_limit_bytes=60 * 1024 * 1024
        ),
    )(record, weights, cot)
    return dx.astype(BF16)[None], dw


def solution(mesh):
    nx = mesh.shape["dp"] // 2
    ny = nx if mesh.shape["tm"] % nx == 0 else 1
    nz = mesh.shape["tm"] // ny
    return jax.shard_map(
        functools.partial(shards, nz, ny, nx),
        mesh=mesh,
        in_specs=(P("dp", "tm", None), P(), P("dp", "tm", None)),
        out_specs=(P("dp", "tm", None), P("tm", None)),
        check_vma=False,
    )
```

```python
import functools

import jax
import jax.numpy as jnp
from jax import lax
from jax.experimental import pallas as pl
from jax.experimental.pallas import tpu as pltpu
from jax.sharding import PartitionSpec as P

H = 4
HD = 128
CH = 256
MESH = pl.DeviceIdType.MESH
F32 = jnp.float32
BF16 = jnp.bfloat16
NN = (((1,), (0,)), ((), ()))
NT = (((1,), (1,)), ((), ()))
TN = (((0,), (0,)), ((), ()))


def mm(a, b, dims=NN):
    return lax.dot_general(a, b, dims, preferred_element_type=F32)


FIRST = ((0, 0), (0, 1), (0, 2))
SECOND = ((1, 0), (1, 1), (1, 2))


def kernel(
    sizes,
    x_hbm, w_hbm, og_hbm, dx_ref, dw_ref,
    x_ref, w_ref, og_ref, in_sem, dcat, qkv, sc, kvg, qgg, loc, dqkv, xt, dxs, dx_sem,
    kst, qst, kyr, qyr,
    part, crecv, a_xr, a_yr, a2, a_zr, ga, b_yr, b_zr, b2, b_xr, b3, gb,
    zk_s, zk_r, zq_s, zq_r, yk_s, yk_r, yq_s, yq_r,
    c_s, c_r, ax_s, ax_r, ay_s, ay_r, az_s, az_r, ag_s, ag_r, af_s, af_r,
    by_s, by_r, bz_s, bz_r, bx_s, bx_r, gb_s, gb_r,
):
    nz, ny, nx = sizes
    tok = x_ref.shape[0]
    nb = tok // CH
    width = H * HD
    rx = dw_ref.shape[0] // nx
    dm = x_ref.shape[1]
    tm, dp = lax.axis_index("tm"), lax.axis_index("dp")
    z, y = tm // ny, lax.rem(tm, ny)
    x, c = dp // 2, lax.rem(dp, 2)

    def at(z_=None, y_=None, x_=None, c_=None):
        z_ = z if z_ is None else z_
        y_ = y if y_ is None else y_
        x_ = x if x_ is None else x_
        c_ = c if c_ is None else c_
        return (z_ * ny + y_, x_ * 2 + c_)

    def zpeer(d):
        return lax.rem(z + d, nz)

    def ypeer(d):
        return lax.rem(y + d, ny)

    def xpeer(d):
        return lax.rem(x + d, nx)

    def remote(src, dst, send, recv, device):
        return pltpu.make_async_remote_copy(
            src_ref=src, dst_ref=dst, send_sem=send, recv_sem=recv,
            device_id=device, device_id_type=MESH,
        )

    def head(p):
        return 2 * lax.rem(p + 1 - c, 2) + p // 2

    peers = [at(c_=1 - c)]
    for d in range(1, nx):
        peers += [at(x_=xpeer(d))]
    peers += [at(y_=ypeer(d)) for d in range(1, ny)]
    peers += [at(z_=zpeer(d)) for d in range(1, nz)]
    barrier = pltpu.get_barrier_semaphore()
    for peer in peers:
        pl.semaphore_signal(barrier, inc=1, device_id=peer, device_id_type=MESH)

    tile = 2 * HD
    tiles = 3 * width // tile

    def weight_copy(i):
        cols = pl.ds(pl.multiple_of(i * tile, tile), tile)
        return pltpu.make_async_copy(w_hbm.at[:, cols], w_ref.at[:, cols], in_sem.at[i])

    x_copy = pltpu.make_async_copy(x_hbm, x_ref, in_sem.at[tiles])
    og_copy = pltpu.make_async_copy(og_hbm, og_ref, in_sem.at[tiles + 1])
    x_copy.start()
    for i in range(tiles):
        weight_copy(i).start()
    og_copy.start()
    x_copy.wait()

    def project(i, carry):
        weight_copy(i).wait()
        r = mm(x_ref[...], w_ref[:, pl.ds(pl.multiple_of(i * tile, tile), tile)]).astype(BF16)
        j, pair = i // (H // 2), lax.rem(i, H // 2)
        qkv[j, 2 * pair] = r[:, :HD]
        qkv[j, 2 * pair + 1] = r[:, HD:]
        return carry

    lax.fori_loop(0, tiles, project, 0)
    og_copy.wait()

    def sums(n, carry):
        rows = pl.ds(pl.multiple_of(n * CH, CH), CH)
        pos = tm * tok + n * CH + lax.broadcasted_iota(jnp.int32, (CH, 1), 0)
        factor = 1.0 / jnp.sqrt(jnp.float32(HD) * (pos.astype(F32) + 1.0))
        g = (og_ref[rows, :].astype(F32) * factor).astype(BF16)
        for h in range(H):
            sg = g[:, h * HD : (h + 1) * HD]
            sc[h, rows, :] = sg
            kvg[n, h] = mm(qkv[1, h, rows, :], qkv[2, h, rows, :], TN)
            qgg[n, h] = mm(qkv[0, h, rows, :], sg, TN)
        return carry

    lax.fori_loop(0, nb, sums, 0)

    pl.semaphore_wait(barrier, len(peers))

    @pl.when(z == 0)
    def _():
        kst[0] = jnp.zeros_like(kst[0])

    @pl.when(z == nz - 1)
    def _():
        qst[0] = jnp.zeros_like(qst[0])

    def link(p, ord_, last, nxt, st, grp, zs, zr, ys, yr_, ybuf, later):
        @pl.when(ord_ > 0)
        def _():
            remote(st.at[1, p], st.at[0, p], zs.at[p], zr.at[p], at(z_=z)).wait_recv()

        hh = head(p)
        total = st[0, p]
        for n in range(nb):
            total = total + grp[n, hh]
        st[1, p] = total

        @pl.when(ord_ < nz - 1)
        def _():
            remote(st.at[1, p], st.at[0, p], zs.at[p], zr.at[p], at(z_=nxt)).start()

        for d in range(1, ny):
            other = ypeer(d)
            which = jnp.where(later(other), 1, 0)
            remote(
                st.at[which, p], ybuf.at[d - 1, p], ys.at[d - 1, p], yr_.at[d - 1, p],
                at(y_=other),
            ).start()

    def local(n, p):
        hh = head(p)
        rows = pl.ds(pl.multiple_of(n * CH, CH), CH)
        q, k, v, s = qkv[0, hh, rows, :], qkv[1, hh, rows, :], qkv[2, hh, rows, :], sc[hh, rows, :]
        row = lax.broadcasted_iota(jnp.int32, (CH, CH), 0)
        col = lax.broadcasted_iota(jnp.int32, (CH, CH), 1)
        low, up = row >= col, row <= col
        vg = jnp.where(low, mm(s, v, NT), 0.0).astype(BF16)
        vgt = jnp.where(up, mm(v, s, NT), 0.0).astype(BF16)
        qkt = jnp.where(up, mm(k, q, NT), 0.0).astype(BF16)
        loc[0, p, rows, :] = mm(vg, k)
        loc[1, p, rows, :] = mm(vgt, q)
        loc[2, p, rows, :] = mm(qkt, s)

    def core_copy(slot, j):
        return remote(part.at[2 * slot, j], crecv.at[slot, j], c_s.at[slot, j], c_r.at[slot, j], at(c_=1 - c))

    def mine(g):
        return part.at[2 * g[0] + 1, g[1]]

    def ax_copy(d, a):
        o = xpeer(d)
        return remote(
            mine(FIRST[a]).at[:, :, o], a_xr.at[d - 1, a], ax_s.at[d - 1, a], ax_r.at[d - 1, a], at(x_=o)
        )

    def ay_copy(d, a):
        o = ypeer(d)
        return remote(
            mine(FIRST[a]).at[:, o, x], a_yr.at[d - 1, a], ay_s.at[d - 1, a], ay_r.at[d - 1, a], at(y_=o)
        )

    def az_copy(d, a):
        o = zpeer(d)
        return remote(a2.at[a, o], a_zr.at[d - 1, a], az_s.at[d - 1, a], az_r.at[d - 1, a], at(z_=o))

    def by_copy(d, b):
        o = ypeer(d)
        return remote(
            mine(SECOND[b]).at[:, o], b_yr.at[d - 1, b], by_s.at[d - 1, b], by_r.at[d - 1, b], at(y_=o)
        )

    def bz_copy(d, b):
        o = zpeer(d)
        return remote(
            mine(SECOND[b]).at[o, y], b_zr.at[d - 1, b], bz_s.at[d - 1, b], bz_r.at[d - 1, b], at(z_=o)
        )

    def bx_copy(d, b):
        o = xpeer(d)
        return remote(b2.at[b], b_xr.at[d - 1, b], bx_s.at[d - 1, b], bx_r.at[d - 1, b], at(x_=o))

    def gb_copy(b):
        return remote(b3.at[b], gb.at[b], gb_s.at[b], gb_r.at[b], at(c_=1 - c))

    def ag_copy(d, a):
        return remote(
            ga.at[0, 0, a], ga.at[0, d, a], ag_s.at[d - 1, a], ag_r.at[d - 1, a], at(x_=xpeer(d))
        )

    def af_copy(d, a):
        return remote(ga.at[0, d, a], ga.at[1, d, a], af_s.at[d, a], af_r.at[d, a], at(c_=1 - c))

    def finish(p):
        hh = head(p)
        start, end = kst[0, p], qst[0, p]
        for d in range(1, ny):
            remote(kst.at[0, p], kyr.at[d - 1, p], yk_s.at[d - 1, p], yk_r.at[d - 1, p], at(y_=ypeer(d))).wait_recv()
            remote(qst.at[0, p], qyr.at[d - 1, p], yq_s.at[d - 1, p], yq_r.at[d - 1, p], at(y_=ypeer(d))).wait_recv()
            start = start + kyr[d - 1, p]
            end = end + qyr[d - 1, p]
        cols = [pl.ds(pl.multiple_of(j * width + hh * HD, HD), HD) for j in range(3)]
        for n in range(nb):
            rows = pl.ds(n * CH, CH)
            dq = loc[0, p, rows, :] + mm(sc[hh, rows, :], start.astype(BF16), NT)
            dqkv[rows, cols[0]] = dq.astype(BF16)
            dcat[rows, :HD] = dq.astype(BF16)
            start = start + kvg[n, hh]
        for n in range(nb - 1, -1, -1):
            rows = pl.ds(n * CH, CH)
            after = end.astype(BF16)
            dk = loc[1, p, rows, :] + mm(qkv[2, hh, rows, :], after, NT)
            dv = loc[2, p, rows, :] + mm(qkv[1, hh, rows, :], after)
            dqkv[rows, cols[1]] = dk.astype(BF16)
            dqkv[rows, cols[2]] = dv.astype(BF16)
            dcat[rows, HD : 2 * HD] = dk.astype(BF16)
            dcat[rows, 2 * HD :] = dv.astype(BF16)
            end = end + qgg[n, hh]
        zb = 2 if nz % 2 == 0 else 1
        m = zb * (dm // nz)

        def slab(i, carry):
            rows = pl.ds(pl.multiple_of(i * m, m), m)
            r = mm(xt[rows, :], dcat[...])
            for j in range(3):
                part[p, j, pl.ds(i * zb, zb)] = r[:, j * HD : (j + 1) * HD].reshape(zb, ny, nx, rx, HD)
            return carry

        lax.fori_loop(0, nz // zb, slab, 0)

    def head_step(p):
        finish(p)
        slot = p // 2

        @pl.when(lax.rem(p, 2) == 0)
        def _():
            for j in range(3):
                core_copy(slot, j).start()

        @pl.when(lax.rem(p, 2) == 1)
        def _():
            for j in range(3):
                core_copy(slot, j).wait_recv()
                for i in range(nz):
                    part[p, j, i] = part[p, j, i] + crecv[slot, j, i]
                for s_ in range(2):

                    @pl.when(slot == s_)
                    def _():
                        if (s_, j) in FIRST:
                            for d in range(1, nx):
                                ax_copy(d, FIRST.index((s_, j))).start()
                        else:
                            for d in range(1, ny):
                                by_copy(d, SECOND.index((s_, j))).start()

    items = nb * (H + 1)
    per = 1
    while any((nz + p + 1) * per < nb * (p + 2) for p in range(H)):
        per += 1

    def step(i, carry):
        kp = i - z
        qp = i - (nz - 1 - z)

        @pl.when((kp >= 0) & (kp < H))
        def _():
            link(kp, z, nz, z + 1, kst, kvg, zk_s, zk_r, yk_s, yk_r, kyr, lambda o: o > y)

        @pl.when((qp >= 0) & (qp < H))
        def _():
            link(qp, nz - 1 - z, nz, z - 1, qst, qgg, zq_s, zq_r, yq_s, yq_r, qyr, lambda o: o < y)

        def piece(u, carry):
            idx = i * per + u
            group, n = idx // nb, lax.rem(idx, nb)

            @pl.when((idx < items) & (group != 1))
            def _():
                local(n, jnp.where(group == 0, 0, group - 1))

            @pl.when(group == 1)
            def _():
                rows = pl.ds(pl.multiple_of(n * CH, CH), CH)
                xt[:, rows] = x_ref[rows, :].T

            return carry

        lax.fori_loop(0, per, piece, 0)

        @pl.when(i >= nz)
        def _():
            head_step(i - nz)

        return carry

    lax.fori_loop(0, nz + H, step, 0)

    out_copy = pltpu.make_async_copy(dxs, dx_ref, dx_sem)

    def rows_of(i):
        cols = pl.ds(i * tile, tile)
        dxs[:, cols] = mm(dqkv[...], w_ref[cols, :], NT).astype(BF16)
        if (i + 1) * tile == dm:
            out_copy.start()

    def a_one(a):
        for d in range(1, nx):
            ax_copy(d, a).wait_recv()
        own = mine(FIRST[a])
        for i in range(nz):
            t = own[i, :, x]
            for d in range(1, nx):
                t = t + a_xr[d - 1, a, i]
            own[i, :, x] = t
        for d in range(1, ny):
            ay_copy(d, a).start()

    def a_two(a):
        for d in range(1, ny):
            ay_copy(d, a).wait_recv()
        own = mine(FIRST[a])
        for i in range(nz):
            t = own[i, y, x]
            for d in range(1, ny):
                t = t + a_yr[d - 1, a, i]
            a2[a, i] = t
        for d in range(1, nz):
            az_copy(d, a).start()

    def a_three(a):
        for d in range(1, nz):
            az_copy(d, a).wait_recv()
        t = a2[a, z]
        for d in range(1, nz):
            t = t + a_zr[d - 1, a]
        ga[0, 0, a] = t
        for d in range(1, nx):
            ag_copy(d, a).start()
        af_copy(0, a).start()

    def cols_of(g, core):
        return pl.ds(pl.multiple_of(g[1] * width + (2 * core + g[0]) * HD, HD), HD)

    def place(flip, d, a):
        rows = pl.ds(pl.multiple_of(lax.rem(x - d + nx, nx) * rx, rx), rx)
        dw_ref[rows, cols_of(FIRST[a], 1 - c if flip else c)] = ga[flip, d, a]

    def a_four(a):
        for d in range(1, nx):
            ag_copy(d, a).wait_recv()
            af_copy(d, a).start()
        for d in range(nx):
            place(0, d, a)

    def a_last(a):
        for d in range(nx):
            af_copy(d, a).wait_recv()
            place(1, d, a)

    def b_one(b):
        for d in range(1, ny):
            by_copy(d, b).wait_recv()
        own = mine(SECOND[b])
        for i in range(nz):
            t = own[i, y]
            for d in range(1, ny):
                t = t + b_yr[d - 1, b, i]
            own[i, y] = t
        for d in range(1, nz):
            bz_copy(d, b).start()

    def b_two(b):
        for d in range(1, nz):
            bz_copy(d, b).wait_recv()
        t = mine(SECOND[b])[z, y]
        for d in range(1, nz):
            t = t + b_zr[d - 1, b]
        b2[b] = t
        for d in range(1, nx):
            bx_copy(d, b).start()

    def b_three(b):
        for d in range(1, nx):
            bx_copy(d, b).wait_recv()
        t = b2[b]
        for d in range(1, nx):
            t = t + b_xr[d - 1, b]
        b3[b] = t
        gb_copy(b).start()
        dw_ref[:, cols_of(SECOND[b], c)] = t.reshape(nx * rx, HD)

    def b_last(b):
        gb_copy(b).wait_recv()
        dw_ref[:, cols_of(SECOND[b], 1 - c)] = gb[b].reshape(nx * rx, HD)

    order = [(a_one, 0)] + [(rows_of, i) for i in range(dm // tile)]
    order += [
        (a_one, 1), (b_one, 0), (a_one, 2), (a_two, 0), (b_one, 1), (a_two, 1), (b_two, 0),
        (b_one, 2), (a_two, 2), (b_two, 1), (b_three, 0), (a_three, 0), (b_two, 2), (b_three, 1),
        (a_three, 1), (a_four, 0), (a_three, 2), (b_three, 2), (a_four, 1), (a_four, 2),
        (b_last, 0), (b_last, 1), (b_last, 2), (a_last, 0), (a_last, 1), (a_last, 2),
    ]
    for work, i in order:
        work(i)
    out_copy.wait()

    def drain_state(p, carry):
        @pl.when(z < nz - 1)
        def _():
            remote(kst.at[1, p], kst.at[0, p], zk_s.at[p], zk_r.at[p], at(z_=z)).wait_send()

        @pl.when(z > 0)
        def _():
            remote(qst.at[1, p], qst.at[0, p], zq_s.at[p], zq_r.at[p], at(z_=z)).wait_send()

        for d in range(1, ny):
            remote(kst.at[0, p], kyr.at[d - 1, p], yk_s.at[d - 1, p], yk_r.at[d - 1, p], at(y_=ypeer(d))).wait_send()
            remote(qst.at[0, p], qyr.at[d - 1, p], yq_s.at[d - 1, p], yq_r.at[d - 1, p], at(y_=ypeer(d))).wait_send()
        return carry

    lax.fori_loop(0, H, drain_state, 0)
    for j in range(3):
        core_copy(0, j).wait_send()
        core_copy(1, j).wait_send()
    for a in range(len(FIRST)):
        for d in range(1, nx):
            ax_copy(d, a).wait_send()
        for d in range(1, ny):
            ay_copy(d, a).wait_send()
        for d in range(1, nz):
            az_copy(d, a).wait_send()
        for d in range(1, nx):
            ag_copy(d, a).wait_send()
        for d in range(nx):
            af_copy(d, a).wait_send()
    for b in range(len(SECOND)):
        for d in range(1, ny):
            by_copy(d, b).wait_send()
        for d in range(1, nz):
            bz_copy(d, b).wait_send()
        for d in range(1, nx):
            bx_copy(d, b).wait_send()
        gb_copy(b).wait_send()


PIECES = 8


def hand_over(dx_ref, dw_ref, dx_out, dw_out, sem):
    m = dx_ref.shape[0] // PIECES
    copies = [
        pltpu.make_async_copy(
            dx_ref.at[pl.ds(i * m, m), :], dx_out.at[0, pl.ds(i * m, m), :], sem.at[i]
        )
        for i in range(PIECES)
    ]
    copies.append(pltpu.make_async_copy(dw_ref, dw_out, sem.at[PIECES]))
    for copy in copies:
        copy.start()
    for copy in copies:
        copy.wait()


def shards(nz, ny, nx, inputs, weights, out_grad):
    record, cot = inputs[0], out_grad[0]
    tok, dm = record.shape
    nb = tok // CH
    rx = dm // (nz * ny * nx)
    na, ns = len(FIRST), len(SECOND)
    V = pltpu.VMEM
    D = pltpu.SemaphoreType.DMA
    scratch = [
        V((tok, dm), BF16), V(weights.shape, BF16), V(cot.shape, BF16), D((3 * H // 2 + 2,)), V((tok, 3 * HD), BF16),
        V((3, H, tok, HD), BF16), V((H, tok, HD), BF16),
        V((nb, H, HD, HD), F32), V((nb, H, HD, HD), F32),
        V((3, H, tok, HD), F32), V((tok, 3 * H * HD), BF16), V((dm, tok), BF16),
        V((tok, dm), BF16), D(()),
        V((2, H, HD, HD), F32), V((2, H, HD, HD), F32),
        V((ny - 1, H, HD, HD), F32), V((ny - 1, H, HD, HD), F32),
        V((4, 3, nz, ny, nx, rx, HD), F32), V((2, 3, nz, ny, nx, rx, HD), F32),
        V((nx - 1, na, nz, ny, rx, HD), F32), V((ny - 1, na, nz, rx, HD), F32),
        V((na, nz, rx, HD), F32), V((nz - 1, na, rx, HD), F32), V((2, nx, na, rx, HD), F32),
        V((ny - 1, ns, nz, nx, rx, HD), F32), V((nz - 1, ns, nx, rx, HD), F32),
        V((ns, nx, rx, HD), F32), V((nx - 1, ns, nx, rx, HD), F32),
        V((ns, nx, rx, HD), F32), V((ns, nx, rx, HD), F32),
        D((H,)), D((H,)), D((H,)), D((H,)),
        D((ny - 1, H)), D((ny - 1, H)), D((ny - 1, H)), D((ny - 1, H)),
        D((2, 3)), D((2, 3)), D((nx - 1, na)), D((nx - 1, na)), D((ny - 1, na)), D((ny - 1, na)),
        D((nz - 1, na)), D((nz - 1, na)), D((nx - 1, na)), D((nx - 1, na)), D((nx, na)), D((nx, na)),
        D((ny - 1, ns)), D((ny - 1, ns)), D((nz - 1, ns)), D((nz - 1, ns)),
        D((nx - 1, ns)), D((nx - 1, ns)), D((ns,)), D((ns,)),
    ]
    vm = pl.BlockSpec(memory_space=pltpu.VMEM)
    hbm = pl.BlockSpec(memory_space=pl.ANY)
    dx, dw = pl.pallas_call(
        functools.partial(kernel, (nz, ny, nx)),
        out_shape=(
            jax.ShapeDtypeStruct((tok, dm), BF16),
            jax.ShapeDtypeStruct((dm // (nz * ny), weights.shape[1]), F32),
        ),
        in_specs=[hbm, hbm, hbm],
        out_specs=(hbm, vm),
        scratch_shapes=scratch,
        compiler_params=pltpu.CompilerParams(
            collective_id=0, has_side_effects=True, vmem_limit_bytes=60 * 1024 * 1024
        ),
    )(record, weights, cot)
    return pl.pallas_call(
        hand_over,
        out_shape=(jax.ShapeDtypeStruct((1, tok, dm), BF16), jax.ShapeDtypeStruct(dw.shape, F32)),
        in_specs=[hbm, hbm],
        out_specs=(hbm, hbm),
        scratch_shapes=[D((PIECES + 1,))],
    )(dx, dw)


def solution(mesh):
    nx = mesh.shape["dp"] // 2
    ny = nx if mesh.shape["tm"] % nx == 0 else 1
    nz = mesh.shape["tm"] // ny
    return jax.shard_map(
        functools.partial(shards, nz, ny, nx),
        mesh=mesh,
        in_specs=(P("dp", "tm", None), P(), P("dp", "tm", None)),
        out_specs=(P("dp", "tm", None), P("tm", None)),
        check_vma=False,
    )
```

```python
import functools

import jax
import jax.numpy as jnp
from jax import lax
from jax.experimental import pallas as pl
from jax.experimental.pallas import tpu as pltpu
from jax.sharding import PartitionSpec as P

H = 4
HD = 128
CH = 256
MESH = pl.DeviceIdType.MESH
F32 = jnp.float32
BF16 = jnp.bfloat16
NN = (((1,), (0,)), ((), ()))
NT = (((1,), (1,)), ((), ()))
TN = (((0,), (0,)), ((), ()))


def mm(a, b, dims=NN):
    return lax.dot_general(a, b, dims, preferred_element_type=F32)


GROUPS = tuple((slot, j) for slot in range(2) for j in range(3))


def kernel(
    sizes,
    x_ref, w_ref, og_ref, dx_ref, dw_ref,
    dcat, qkv, sc, kvg, qgg, loc, dqkv, xt, dxs, dx_sem,
    kst, qst, kyr, qyr,
    part, crecv, a_xr, a_yr, a2, a_zr, ga, b_yr, b_zr, b2, b_xr, b3, gb,
    zk_s, zk_r, zq_s, zq_r, yk_s, yk_r, yq_s, yq_r,
    c_s, c_r, ax_s, ax_r, ay_s, ay_r, az_s, az_r, ag_s, ag_r, af_s, af_r,
    by_s, by_r, bz_s, bz_r, bx_s, bx_r, gb_s, gb_r,
):
    nz, ny, nx = sizes
    tok = x_ref.shape[0]
    nb = tok // CH
    width = H * HD
    rx = dw_ref.shape[0] // nx
    dm = x_ref.shape[1]
    tm, dp = lax.axis_index("tm"), lax.axis_index("dp")
    z, y = tm // ny, lax.rem(tm, ny)
    x, c = dp // 2, lax.rem(dp, 2)

    def at(z_=None, y_=None, x_=None, c_=None):
        z_ = z if z_ is None else z_
        y_ = y if y_ is None else y_
        x_ = x if x_ is None else x_
        c_ = c if c_ is None else c_
        return (z_ * ny + y_, x_ * 2 + c_)

    def zpeer(d):
        return lax.rem(z + d, nz)

    def ypeer(d):
        return lax.rem(y + d, ny)

    def xpeer(d):
        return lax.rem(x + d, nx)

    def remote(src, dst, send, recv, device):
        return pltpu.make_async_remote_copy(
            src_ref=src, dst_ref=dst, send_sem=send, recv_sem=recv,
            device_id=device, device_id_type=MESH,
        )

    def head(p):
        return 2 * lax.rem(p + 1 - c, 2) + p // 2

    peers = [at(c_=1 - c)]
    for d in range(1, nx):
        peers += [at(x_=xpeer(d))]
    peers += [at(y_=ypeer(d)) for d in range(1, ny)]
    peers += [at(z_=zpeer(d)) for d in range(1, nz)]
    barrier = pltpu.get_barrier_semaphore()
    for peer in peers:
        pl.semaphore_signal(barrier, inc=1, device_id=peer, device_id_type=MESH)

    def project(n, carry):
        rows = pl.ds(pl.multiple_of(n * CH, CH), CH)
        r = mm(x_ref[rows, :], w_ref[...]).astype(BF16)
        pos = tm * tok + n * CH + lax.broadcasted_iota(jnp.int32, (CH, 1), 0)
        factor = 1.0 / jnp.sqrt(jnp.float32(HD) * (pos.astype(F32) + 1.0))
        g = (og_ref[rows, :].astype(F32) * factor).astype(BF16)
        for h in range(H):
            q = r[:, h * HD : (h + 1) * HD]
            k = r[:, width + h * HD : width + (h + 1) * HD]
            v = r[:, 2 * width + h * HD : 2 * width + (h + 1) * HD]
            s = g[:, h * HD : (h + 1) * HD]
            qkv[0, h, rows, :] = q
            qkv[1, h, rows, :] = k
            qkv[2, h, rows, :] = v
            sc[h, rows, :] = s
            kvg[n, h] = mm(k, v, TN)
            qgg[n, h] = mm(q, s, TN)
        return carry

    lax.fori_loop(0, nb, project, 0)

    pl.semaphore_wait(barrier, len(peers))

    @pl.when(z == 0)
    def _():
        kst[0] = jnp.zeros_like(kst[0])

    @pl.when(z == nz - 1)
    def _():
        qst[0] = jnp.zeros_like(qst[0])

    def link(p, ord_, last, nxt, st, grp, zs, zr, ys, yr_, ybuf, later):
        @pl.when(ord_ > 0)
        def _():
            remote(st.at[1, p], st.at[0, p], zs.at[p], zr.at[p], at(z_=z)).wait_recv()

        hh = head(p)
        total = st[0, p]
        for n in range(nb):
            total = total + grp[n, hh]
        st[1, p] = total

        @pl.when(ord_ < nz - 1)
        def _():
            remote(st.at[1, p], st.at[0, p], zs.at[p], zr.at[p], at(z_=nxt)).start()

        for d in range(1, ny):
            other = ypeer(d)
            which = jnp.where(later(other), 1, 0)
            remote(
                st.at[which, p], ybuf.at[d - 1, p], ys.at[d - 1, p], yr_.at[d - 1, p],
                at(y_=other),
            ).start()

    def local(n, p):
        hh = head(p)
        rows = pl.ds(pl.multiple_of(n * CH, CH), CH)
        q, k, v, s = qkv[0, hh, rows, :], qkv[1, hh, rows, :], qkv[2, hh, rows, :], sc[hh, rows, :]
        row = lax.broadcasted_iota(jnp.int32, (CH, CH), 0)
        col = lax.broadcasted_iota(jnp.int32, (CH, CH), 1)
        low, up = row >= col, row <= col
        vg = jnp.where(low, mm(s, v, NT), 0.0).astype(BF16)
        vgt = jnp.where(up, mm(v, s, NT), 0.0).astype(BF16)
        qkt = jnp.where(up, mm(k, q, NT), 0.0).astype(BF16)
        loc[0, p, rows, :] = mm(vg, k)
        loc[1, p, rows, :] = mm(vgt, q)
        loc[2, p, rows, :] = mm(qkt, s)

    def core_copy(slot, j):
        return remote(part.at[2 * slot, j], crecv.at[slot, j], c_s.at[slot, j], c_r.at[slot, j], at(c_=1 - c))

    def mine(g):
        return part.at[2 * g[0] + 1, g[1]]

    def ax_copy(d, a):
        o = xpeer(d)
        return remote(
            mine(GROUPS[a]).at[:, :, o], a_xr.at[d - 1, a], ax_s.at[d - 1, a], ax_r.at[d - 1, a], at(x_=o)
        )

    def ay_copy(d, a):
        o = ypeer(d)
        return remote(
            mine(GROUPS[a]).at[:, o, x], a_yr.at[d - 1, a], ay_s.at[d - 1, a], ay_r.at[d - 1, a], at(y_=o)
        )

    def az_copy(d, a):
        o = zpeer(d)
        return remote(a2.at[a, o], a_zr.at[d - 1, a], az_s.at[d - 1, a], az_r.at[d - 1, a], at(z_=o))

    def by_copy(d, b):
        o = ypeer(d)
        return remote(
            mine(GROUPS[b]).at[:, o], b_yr.at[d - 1, b], by_s.at[d - 1, b], by_r.at[d - 1, b], at(y_=o)
        )

    def bz_copy(d, b):
        o = zpeer(d)
        return remote(
            mine(GROUPS[b]).at[o, y], b_zr.at[d - 1, b], bz_s.at[d - 1, b], bz_r.at[d - 1, b], at(z_=o)
        )

    def bx_copy(d, b):
        o = xpeer(d)
        return remote(b2.at[b], b_xr.at[d - 1, b], bx_s.at[d - 1, b], bx_r.at[d - 1, b], at(x_=o))

    def gb_copy(b):
        return remote(b3.at[b], gb.at[b], gb_s.at[b], gb_r.at[b], at(c_=1 - c))

    def ag_copy(d, a):
        return remote(
            ga.at[0, 0, a], ga.at[0, d, a], ag_s.at[d - 1, a], ag_r.at[d - 1, a], at(x_=xpeer(d))
        )

    def af_copy(d, a):
        return remote(ga.at[0, d, a], ga.at[1, d, a], af_s.at[d, a], af_r.at[d, a], at(c_=1 - c))

    def finish(p):
        hh = head(p)
        start, end = kst[0, p], qst[0, p]
        for d in range(1, ny):
            remote(kst.at[0, p], kyr.at[d - 1, p], yk_s.at[d - 1, p], yk_r.at[d - 1, p], at(y_=ypeer(d))).wait_recv()
            remote(qst.at[0, p], qyr.at[d - 1, p], yq_s.at[d - 1, p], yq_r.at[d - 1, p], at(y_=ypeer(d))).wait_recv()
            start = start + kyr[d - 1, p]
            end = end + qyr[d - 1, p]
        cols = [pl.ds(pl.multiple_of(j * width + hh * HD, HD), HD) for j in range(3)]
        for n in range(nb):
            rows = pl.ds(n * CH, CH)
            dq = loc[0, p, rows, :] + mm(sc[hh, rows, :], start.astype(BF16), NT)
            dqkv[rows, cols[0]] = dq.astype(BF16)
            dcat[rows, :HD] = dq.astype(BF16)
            start = start + kvg[n, hh]
        for n in range(nb - 1, -1, -1):
            rows = pl.ds(n * CH, CH)
            after = end.astype(BF16)
            dk = loc[1, p, rows, :] + mm(qkv[2, hh, rows, :], after, NT)
            dv = loc[2, p, rows, :] + mm(qkv[1, hh, rows, :], after)
            dqkv[rows, cols[1]] = dk.astype(BF16)
            dqkv[rows, cols[2]] = dv.astype(BF16)
            dcat[rows, HD : 2 * HD] = dk.astype(BF16)
            dcat[rows, 2 * HD :] = dv.astype(BF16)
            end = end + qgg[n, hh]
        zb = 2 if nz % 2 == 0 else 1
        m = zb * (dm // nz)

        def slab(i, carry):
            rows = pl.ds(pl.multiple_of(i * m, m), m)
            r = mm(xt[rows, :], dcat[...])
            for j in range(3):
                part[p, j, pl.ds(i * zb, zb)] = r[:, j * HD : (j + 1) * HD].reshape(zb, ny, nx, rx, HD)
            return carry

        lax.fori_loop(0, nz // zb, slab, 0)

    def head_step(p):
        finish(p)
        slot = p // 2

        @pl.when(lax.rem(p, 2) == 0)
        def _():
            for j in range(3):
                core_copy(slot, j).start()

        @pl.when(lax.rem(p, 2) == 1)
        def _():
            for j in range(3):
                core_copy(slot, j).wait_recv()
                for i in range(nz):
                    part[p, j, i] = part[p, j, i] + crecv[slot, j, i]
                for s_ in range(2):

                    @pl.when((slot == s_) & (c == 0))
                    def _():
                        for d in range(1, nx):
                            ax_copy(d, GROUPS.index((s_, j))).start()

                    @pl.when((slot == s_) & (c == 1))
                    def _():
                        for d in range(1, ny):
                            by_copy(d, GROUPS.index((s_, j))).start()

    items = nb * (H + 1)
    per = 1
    while any((nz + p + 1) * per < nb * (p + 2) for p in range(H)):
        per += 1

    def step(i, carry):
        kp = i - z
        qp = i - (nz - 1 - z)

        @pl.when((kp >= 0) & (kp < H))
        def _():
            link(kp, z, nz, z + 1, kst, kvg, zk_s, zk_r, yk_s, yk_r, kyr, lambda o: o > y)

        @pl.when((qp >= 0) & (qp < H))
        def _():
            link(qp, nz - 1 - z, nz, z - 1, qst, qgg, zq_s, zq_r, yq_s, yq_r, qyr, lambda o: o < y)

        def piece(u, carry):
            idx = i * per + u
            group, n = idx // nb, lax.rem(idx, nb)

            @pl.when((idx < items) & (group != 1))
            def _():
                local(n, jnp.where(group == 0, 0, group - 1))

            @pl.when(group == 1)
            def _():
                rows = pl.ds(pl.multiple_of(n * CH, CH), CH)
                xt[:, rows] = x_ref[rows, :].T

            return carry

        lax.fori_loop(0, per, piece, 0)

        @pl.when(i >= nz)
        def _():
            head_step(i - nz)

        return carry

    lax.fori_loop(0, nz + H, step, 0)

    def out_copy(i):
        rows = pl.ds(i * CH, CH)
        return pltpu.make_async_copy(dxs.at[rows, :], dx_ref.at[rows, :], dx_sem.at[i])

    def rows_of(i):
        rows = pl.ds(i * CH, CH)
        dxs[rows, :] = mm(dqkv[rows, :], w_ref[...], NT).astype(BF16)
        out_copy(i).start()

    def a_one(a):
        for d in range(1, nx):
            ax_copy(d, a).wait_recv()
        own = mine(GROUPS[a])
        for i in range(nz):
            t = own[i, :, x]
            for d in range(1, nx):
                t = t + a_xr[d - 1, a, i]
            own[i, :, x] = t
        for d in range(1, ny):
            ay_copy(d, a).start()

    def a_two(a):
        for d in range(1, ny):
            ay_copy(d, a).wait_recv()
        own = mine(GROUPS[a])
        for i in range(nz):
            t = own[i, y, x]
            for d in range(1, ny):
                t = t + a_yr[d - 1, a, i]
            a2[a, i] = t
        for d in range(1, nz):
            az_copy(d, a).start()

    def a_three(a):
        for d in range(1, nz):
            az_copy(d, a).wait_recv()
        t = a2[a, z]
        for d in range(1, nz):
            t = t + a_zr[d - 1, a]
        ga[0, 0, a] = t
        for d in range(1, nx):
            ag_copy(d, a).start()
        af_copy(0, a).start()

    def cols_of(g, core):
        return pl.ds(pl.multiple_of(g[1] * width + (2 * core + g[0]) * HD, HD), HD)

    def place(flip, d, a):
        rows = pl.ds(pl.multiple_of(lax.rem(x - d + nx, nx) * rx, rx), rx)
        dw_ref[rows, cols_of(GROUPS[a], 0)] = ga[flip, d, a]

    def a_four(a):
        for d in range(1, nx):
            ag_copy(d, a).wait_recv()
            af_copy(d, a).start()
        for d in range(nx):
            place(0, d, a)

    def a_last(a):
        for d in range(nx):
            af_copy(d, a).wait_recv()
            place(1, d, a)

    def b_one(b):
        for d in range(1, ny):
            by_copy(d, b).wait_recv()
        own = mine(GROUPS[b])
        for i in range(nz):
            t = own[i, y]
            for d in range(1, ny):
                t = t + b_yr[d - 1, b, i]
            own[i, y] = t
        for d in range(1, nz):
            bz_copy(d, b).start()

    def b_two(b):
        for d in range(1, nz):
            bz_copy(d, b).wait_recv()
        t = mine(GROUPS[b])[z, y]
        for d in range(1, nz):
            t = t + b_zr[d - 1, b]
        b2[b] = t
        for d in range(1, nx):
            bx_copy(d, b).start()

    def b_three(b):
        for d in range(1, nx):
            bx_copy(d, b).wait_recv()
        t = b2[b]
        for d in range(1, nx):
            t = t + b_xr[d - 1, b]
        b3[b] = t
        gb_copy(b).start()
        dw_ref[:, cols_of(GROUPS[b], 1)] = t.reshape(nx * rx, HD)

    def b_last(b):
        gb_copy(b).wait_recv()
        dw_ref[:, cols_of(GROUPS[b], 1)] = gb[b].reshape(nx * rx, HD)

    count = len(GROUPS)

    def waves(stages, gap):
        order = []
        for w in range(count + gap * len(stages)):
            if w < nb:
                order.append((rows_of, w))
            for lag, stage in enumerate(stages):
                if 0 <= w - gap * lag < count:
                    order.append((stage, w - gap * lag))
        for work, i in order:
            work(i)

    @pl.when(c == 0)
    def _():
        waves((a_one, a_two, a_three, a_four), 1)
        for b in range(count):
            b_last(b)

    @pl.when(c == 1)
    def _():
        waves((b_one, b_two, b_three), 1)
        for a in range(count):
            a_last(a)

    for i in range(nb):
        out_copy(i).wait()

    def drain_state(p, carry):
        @pl.when(z < nz - 1)
        def _():
            remote(kst.at[1, p], kst.at[0, p], zk_s.at[p], zk_r.at[p], at(z_=z)).wait_send()

        @pl.when(z > 0)
        def _():
            remote(qst.at[1, p], qst.at[0, p], zq_s.at[p], zq_r.at[p], at(z_=z)).wait_send()

        for d in range(1, ny):
            remote(kst.at[0, p], kyr.at[d - 1, p], yk_s.at[d - 1, p], yk_r.at[d - 1, p], at(y_=ypeer(d))).wait_send()
            remote(qst.at[0, p], qyr.at[d - 1, p], yq_s.at[d - 1, p], yq_r.at[d - 1, p], at(y_=ypeer(d))).wait_send()
        return carry

    lax.fori_loop(0, H, drain_state, 0)
    for j in range(3):
        core_copy(0, j).wait_send()
        core_copy(1, j).wait_send()

    @pl.when(c == 0)
    def _():
        for a in range(count):
            for d in range(1, nx):
                ax_copy(d, a).wait_send()
                ag_copy(d, a).wait_send()
            for d in range(1, ny):
                ay_copy(d, a).wait_send()
            for d in range(1, nz):
                az_copy(d, a).wait_send()
            for d in range(nx):
                af_copy(d, a).wait_send()

    @pl.when(c == 1)
    def _():
        for b in range(count):
            for d in range(1, ny):
                by_copy(d, b).wait_send()
            for d in range(1, nz):
                bz_copy(d, b).wait_send()
            for d in range(1, nx):
                bx_copy(d, b).wait_send()
            gb_copy(b).wait_send()


def shards(nz, ny, nx, inputs, weights, out_grad):
    record, cot = inputs[0], out_grad[0]
    tok, dm = record.shape
    nb = tok // CH
    rx = dm // (nz * ny * nx)
    na = ns = len(GROUPS)
    V = pltpu.VMEM
    D = pltpu.SemaphoreType.DMA
    scratch = [
        V((tok, 3 * HD), BF16),
        V((3, H, tok, HD), BF16), V((H, tok, HD), BF16),
        V((nb, H, HD, HD), F32), V((nb, H, HD, HD), F32),
        V((3, H, tok, HD), F32), V((tok, 3 * H * HD), BF16), V((dm, tok), BF16),
        V((tok, dm), BF16), D((nb,)),
        V((2, H, HD, HD), F32), V((2, H, HD, HD), F32),
        V((ny - 1, H, HD, HD), F32), V((ny - 1, H, HD, HD), F32),
        V((4, 3, nz, ny, nx, rx, HD), F32), V((2, 3, nz, ny, nx, rx, HD), F32),
        V((nx - 1, na, nz, ny, rx, HD), F32), V((ny - 1, na, nz, rx, HD), F32),
        V((na, nz, rx, HD), F32), V((nz - 1, na, rx, HD), F32), V((2, nx, na, rx, HD), F32),
        V((ny - 1, ns, nz, nx, rx, HD), F32), V((nz - 1, ns, nx, rx, HD), F32),
        V((ns, nx, rx, HD), F32), V((nx - 1, ns, nx, rx, HD), F32),
        V((ns, nx, rx, HD), F32), V((ns, nx, rx, HD), F32),
        D((H,)), D((H,)), D((H,)), D((H,)),
        D((ny - 1, H)), D((ny - 1, H)), D((ny - 1, H)), D((ny - 1, H)),
        D((2, 3)), D((2, 3)), D((nx - 1, na)), D((nx - 1, na)), D((ny - 1, na)), D((ny - 1, na)),
        D((nz - 1, na)), D((nz - 1, na)), D((nx - 1, na)), D((nx - 1, na)), D((nx, na)), D((nx, na)),
        D((ny - 1, ns)), D((ny - 1, ns)), D((nz - 1, ns)), D((nz - 1, ns)),
        D((nx - 1, ns)), D((nx - 1, ns)), D((ns,)), D((ns,)),
    ]
    vm = pl.BlockSpec(memory_space=pltpu.VMEM)
    hbm = pl.BlockSpec(memory_space=pl.ANY)
    dx, dw = pl.pallas_call(
        functools.partial(kernel, (nz, ny, nx)),
        out_shape=(
            jax.ShapeDtypeStruct((tok, dm), BF16),
            jax.ShapeDtypeStruct((dm // (nz * ny), weights.shape[1]), F32),
        ),
        in_specs=[vm, vm, vm],
        out_specs=(hbm, vm),
        scratch_shapes=scratch,
        compiler_params=pltpu.CompilerParams(
            collective_id=0, has_side_effects=True, vmem_limit_bytes=60 * 1024 * 1024
        ),
    )(record, weights, cot)
    return dx[None], dw


def solution(mesh):
    nx = mesh.shape["dp"] // 2
    ny = nx if mesh.shape["tm"] % nx == 0 else 1
    nz = mesh.shape["tm"] // ny
    return jax.shard_map(
        functools.partial(shards, nz, ny, nx),
        mesh=mesh,
        in_specs=(P("dp", "tm", None), P(), P("dp", "tm", None)),
        out_specs=(P("dp", "tm", None), P("tm", None)),
        check_vma=False,
    )
```

```python
import functools

import jax
import jax.numpy as jnp
from jax import lax
from jax.experimental import pallas as pl
from jax.experimental.pallas import tpu as pltpu
from jax.sharding import PartitionSpec as P

H = 4
HD = 128
CH = 256
MESH = pl.DeviceIdType.MESH
F32 = jnp.float32
BF16 = jnp.bfloat16
NN = (((1,), (0,)), ((), ()))
NT = (((1,), (1,)), ((), ()))
TN = (((0,), (0,)), ((), ()))


def mm(a, b, dims=NN):
    return lax.dot_general(a, b, dims, preferred_element_type=F32)


GROUPS = tuple((slot, j) for slot in range(2) for j in range(3))


def kernel(
    sizes,
    x_ref, w_ref, og_ref, dx_ref, dw_ref,
    dcat, qkv, sc, kvg, qgg, loc, dqkv, xt, dxs, dx_sem,
    kst, qst, kyr, qyr,
    part, crecv, a_xr, a_yr, a2, a_zr, ga, b_yr, b_zr, b2, b_xr, b3, gb,
    zk_s, zk_r, zq_s, zq_r, yk_s, yk_r, yq_s, yq_r,
    c_s, c_r, ax_s, ax_r, ay_s, ay_r, az_s, az_r, ag_s, ag_r, af_s, af_r,
    by_s, by_r, bz_s, bz_r, bx_s, bx_r, gb_s, gb_r,
):
    nz, ny, nx = sizes
    tok = x_ref.shape[0]
    nb = tok // CH
    width = H * HD
    rx = dw_ref.shape[0] // nx
    dm = x_ref.shape[1]
    tm, dp = lax.axis_index("tm"), lax.axis_index("dp")
    z, y = tm // ny, lax.rem(tm, ny)
    x, c = dp // 2, lax.rem(dp, 2)

    def at(z_=None, y_=None, x_=None, c_=None):
        z_ = z if z_ is None else z_
        y_ = y if y_ is None else y_
        x_ = x if x_ is None else x_
        c_ = c if c_ is None else c_
        return (z_ * ny + y_, x_ * 2 + c_)

    def zpeer(d):
        return lax.rem(z + d, nz)

    def ypeer(d):
        return lax.rem(y + d, ny)

    def xpeer(d):
        return lax.rem(x + d, nx)

    def remote(src, dst, send, recv, device):
        return pltpu.make_async_remote_copy(
            src_ref=src, dst_ref=dst, send_sem=send, recv_sem=recv,
            device_id=device, device_id_type=MESH,
        )

    def head(p):
        return 2 * lax.rem(p + 1 - c, 2) + p // 2

    peers = [at(c_=1 - c)]
    for d in range(1, nx):
        peers += [at(x_=xpeer(d))]
    peers += [at(y_=ypeer(d)) for d in range(1, ny)]
    peers += [at(z_=zpeer(d)) for d in range(1, nz)]
    barrier = pltpu.get_barrier_semaphore()
    for peer in peers:
        pl.semaphore_signal(barrier, inc=1, device_id=peer, device_id_type=MESH)

    def project(n, carry):
        rows = pl.ds(pl.multiple_of(n * CH, CH), CH)
        r = mm(x_ref[rows, :], w_ref[...]).astype(BF16)
        pos = tm * tok + n * CH + lax.broadcasted_iota(jnp.int32, (CH, 1), 0)
        factor = 1.0 / jnp.sqrt(jnp.float32(HD) * (pos.astype(F32) + 1.0))
        g = (og_ref[rows, :].astype(F32) * factor).astype(BF16)
        for h in range(H):
            q = r[:, h * HD : (h + 1) * HD]
            k = r[:, width + h * HD : width + (h + 1) * HD]
            v = r[:, 2 * width + h * HD : 2 * width + (h + 1) * HD]
            s = g[:, h * HD : (h + 1) * HD]
            qkv[0, h, rows, :] = q
            qkv[1, h, rows, :] = k
            qkv[2, h, rows, :] = v
            sc[h, rows, :] = s
            kvg[n, h] = mm(k, v, TN)
            qgg[n, h] = mm(q, s, TN)
        return carry

    lax.fori_loop(0, nb, project, 0)

    pl.semaphore_wait(barrier, len(peers))

    @pl.when(z == 0)
    def _():
        kst[0] = jnp.zeros_like(kst[0])

    @pl.when(z == nz - 1)
    def _():
        qst[0] = jnp.zeros_like(qst[0])

    def link(p, ord_, last, nxt, st, grp, zs, zr, ys, yr_, ybuf, later):
        @pl.when(ord_ > 0)
        def _():
            remote(st.at[1, p], st.at[0, p], zs.at[p], zr.at[p], at(z_=z)).wait_recv()

        hh = head(p)
        total = st[0, p]
        for n in range(nb):
            total = total + grp[n, hh]
        st[1, p] = total

        @pl.when(ord_ < nz - 1)
        def _():
            remote(st.at[1, p], st.at[0, p], zs.at[p], zr.at[p], at(z_=nxt)).start()

        for d in range(1, ny):
            other = ypeer(d)
            which = jnp.where(later(other), 1, 0)
            remote(
                st.at[which, p], ybuf.at[d - 1, p], ys.at[d - 1, p], yr_.at[d - 1, p],
                at(y_=other),
            ).start()

    def local(n, p):
        hh = head(p)
        rows = pl.ds(pl.multiple_of(n * CH, CH), CH)
        q, k, v, s = qkv[0, hh, rows, :], qkv[1, hh, rows, :], qkv[2, hh, rows, :], sc[hh, rows, :]
        row = lax.broadcasted_iota(jnp.int32, (CH, CH), 0)
        col = lax.broadcasted_iota(jnp.int32, (CH, CH), 1)
        low, up = row >= col, row <= col
        vg = jnp.where(low, mm(s, v, NT), 0.0).astype(BF16)
        vgt = jnp.where(up, mm(v, s, NT), 0.0).astype(BF16)
        qkt = jnp.where(up, mm(k, q, NT), 0.0).astype(BF16)
        loc[0, p, rows, :] = mm(vg, k)
        loc[1, p, rows, :] = mm(vgt, q)
        loc[2, p, rows, :] = mm(qkt, s)

    def core_copy(slot, j):
        return remote(part.at[2 * slot, j], crecv.at[slot, j], c_s.at[slot, j], c_r.at[slot, j], at(c_=1 - c))

    def mine(g):
        return part.at[2 * g[0] + 1, g[1]]

    def ax_copy(d, a):
        o = xpeer(d)
        return remote(
            mine(GROUPS[a]).at[:, :, o], a_xr.at[d - 1, a], ax_s.at[d - 1, a], ax_r.at[d - 1, a], at(x_=o)
        )

    def ay_copy(d, a):
        o = ypeer(d)
        return remote(
            mine(GROUPS[a]).at[:, o, x], a_yr.at[d - 1, a], ay_s.at[d - 1, a], ay_r.at[d - 1, a], at(y_=o)
        )

    def az_copy(d, a):
        o = zpeer(d)
        return remote(a2.at[a, o], a_zr.at[d - 1, a], az_s.at[d - 1, a], az_r.at[d - 1, a], at(z_=o))

    def by_copy(d, b):
        o = ypeer(d)
        return remote(
            mine(GROUPS[b]).at[:, o], b_yr.at[d - 1, b], by_s.at[d - 1, b], by_r.at[d - 1, b], at(y_=o)
        )

    def bz_copy(d, b):
        o = zpeer(d)
        return remote(
            mine(GROUPS[b]).at[o, y], b_zr.at[d - 1, b], bz_s.at[d - 1, b], bz_r.at[d - 1, b], at(z_=o)
        )

    def bx_copy(d, b):
        o = xpeer(d)
        return remote(b2.at[b], b_xr.at[d - 1, b], bx_s.at[d - 1, b], bx_r.at[d - 1, b], at(x_=o))

    def gb_copy(b):
        return remote(b3.at[b], gb.at[b], gb_s.at[b], gb_r.at[b], at(c_=1 - c))

    def ag_copy(d, a):
        return remote(
            ga.at[0, 0, a], ga.at[0, d, a], ag_s.at[d - 1, a], ag_r.at[d - 1, a], at(x_=xpeer(d))
        )

    def af_copy(d, a):
        return remote(ga.at[0, d, a], ga.at[1, d, a], af_s.at[d, a], af_r.at[d, a], at(c_=1 - c))

    def finish(p):
        hh = head(p)
        start, end = kst[0, p], qst[0, p]
        for d in range(1, ny):
            remote(kst.at[0, p], kyr.at[d - 1, p], yk_s.at[d - 1, p], yk_r.at[d - 1, p], at(y_=ypeer(d))).wait_recv()
            remote(qst.at[0, p], qyr.at[d - 1, p], yq_s.at[d - 1, p], yq_r.at[d - 1, p], at(y_=ypeer(d))).wait_recv()
            start = start + kyr[d - 1, p]
            end = end + qyr[d - 1, p]
        cols = [pl.ds(pl.multiple_of(j * width + hh * HD, HD), HD) for j in range(3)]
        for n in range(nb):
            rows = pl.ds(n * CH, CH)
            dq = loc[0, p, rows, :] + mm(sc[hh, rows, :], start.astype(BF16), NT)
            dqkv[rows, cols[0]] = dq.astype(BF16)
            dcat[rows, :HD] = dq.astype(BF16)
            start = start + kvg[n, hh]
        for n in range(nb - 1, -1, -1):
            rows = pl.ds(n * CH, CH)
            after = end.astype(BF16)
            dk = loc[1, p, rows, :] + mm(qkv[2, hh, rows, :], after, NT)
            dv = loc[2, p, rows, :] + mm(qkv[1, hh, rows, :], after)
            dqkv[rows, cols[1]] = dk.astype(BF16)
            dqkv[rows, cols[2]] = dv.astype(BF16)
            dcat[rows, HD : 2 * HD] = dk.astype(BF16)
            dcat[rows, 2 * HD :] = dv.astype(BF16)
            end = end + qgg[n, hh]
        zb = 2 if nz % 2 == 0 else 1
        m = zb * (dm // nz)

        def slab(i, carry):
            rows = pl.ds(pl.multiple_of(i * m, m), m)
            r = mm(xt[rows, :], dcat[...])
            for j in range(3):
                part[p, j, pl.ds(i * zb, zb)] = r[:, j * HD : (j + 1) * HD].reshape(zb, ny, nx, rx, HD)
            return carry

        lax.fori_loop(0, nz // zb, slab, 0)

    def head_step(p):
        finish(p)
        slot = p // 2

        @pl.when(lax.rem(p, 2) == 0)
        def _():
            for j in range(3):
                core_copy(slot, j).start()

        @pl.when(lax.rem(p, 2) == 1)
        def _():
            for j in range(3):
                core_copy(slot, j).wait_recv()
                for i in range(nz):
                    part[p, j, i] = part[p, j, i] + crecv[slot, j, i]
                for s_ in range(2):

                    @pl.when((slot == s_) & (c == 0))
                    def _():
                        for d in range(1, nx):
                            ax_copy(d, GROUPS.index((s_, j))).start()

                    @pl.when((slot == s_) & (c == 1))
                    def _():
                        for d in range(1, ny):
                            by_copy(d, GROUPS.index((s_, j))).start()

    items = nb * (H + 1)
    per = 1
    while any((nz + p + 1) * per < nb * (p + 2) for p in range(H)):
        per += 1

    def step(i, carry):
        kp = i - z
        qp = i - (nz - 1 - z)

        @pl.when((kp >= 0) & (kp < H))
        def _():
            link(kp, z, nz, z + 1, kst, kvg, zk_s, zk_r, yk_s, yk_r, kyr, lambda o: o > y)

        @pl.when((qp >= 0) & (qp < H))
        def _():
            link(qp, nz - 1 - z, nz, z - 1, qst, qgg, zq_s, zq_r, yq_s, yq_r, qyr, lambda o: o < y)

        def piece(u, carry):
            idx = i * per + u
            group, n = idx // nb, lax.rem(idx, nb)

            @pl.when((idx < items) & (group != 1))
            def _():
                local(n, jnp.where(group == 0, 0, group - 1))

            @pl.when(group == 1)
            def _():
                rows = pl.ds(pl.multiple_of(n * CH, CH), CH)
                xt[:, rows] = x_ref[rows, :].T

            return carry

        lax.fori_loop(0, per, piece, 0)

        @pl.when(i >= nz)
        def _():
            head_step(i - nz)

        return carry

    lax.fori_loop(0, nz + H, step, 0)

    def out_copy(i):
        rows = pl.ds(i * CH, CH)
        return pltpu.make_async_copy(dxs.at[rows, :], dx_ref.at[rows, :], dx_sem.at[i])

    def rows_of(i):
        rows = pl.ds(i * CH, CH)
        dxs[rows, :] = mm(dqkv[rows, :], w_ref[...], NT).astype(BF16)
        out_copy(i).start()

    def a_one(a):
        for d in range(1, nx):
            ax_copy(d, a).wait_recv()
        own = mine(GROUPS[a])
        for i in range(nz):
            t = own[i, :, x]
            for d in range(1, nx):
                t = t + a_xr[d - 1, a, i]
            own[i, :, x] = t
        for d in range(1, ny):
            ay_copy(d, a).start()

    def a_two(a):
        for d in range(1, ny):
            ay_copy(d, a).wait_recv()
        own = mine(GROUPS[a])
        for i in range(nz):
            t = own[i, y, x]
            for d in range(1, ny):
                t = t + a_yr[d - 1, a, i]
            a2[a, i] = t
        for d in range(1, nz):
            az_copy(d, a).start()

    def a_three(a):
        for d in range(1, nz):
            az_copy(d, a).wait_recv()
        t = a2[a, z]
        for d in range(1, nz):
            t = t + a_zr[d - 1, a]
        ga[0, 0, a] = t
        for d in range(1, nx):
            ag_copy(d, a).start()
        af_copy(0, a).start()

    def cols_of(g, core):
        return pl.ds(pl.multiple_of(g[1] * width + (2 * core + g[0]) * HD, HD), HD)

    def place(flip, d, a):
        rows = pl.ds(pl.multiple_of(lax.rem(x - d + nx, nx) * rx, rx), rx)
        dw_ref[rows, cols_of(GROUPS[a], 0)] = ga[flip, d, a]

    def a_four(a):
        for d in range(1, nx):
            ag_copy(d, a).wait_recv()
            af_copy(d, a).start()
        for d in range(nx):
            place(0, d, a)

    def a_last(a):
        for d in range(nx):
            af_copy(d, a).wait_recv()
            place(1, d, a)

    def b_one(b):
        for d in range(1, ny):
            by_copy(d, b).wait_recv()
        own = mine(GROUPS[b])
        for i in range(nz):
            t = own[i, y]
            for d in range(1, ny):
                t = t + b_yr[d - 1, b, i]
            own[i, y] = t
        for d in range(1, nz):
            bz_copy(d, b).start()

    def b_two(b):
        for d in range(1, nz):
            bz_copy(d, b).wait_recv()
        t = mine(GROUPS[b])[z, y]
        for d in range(1, nz):
            t = t + b_zr[d - 1, b]
        b2[b] = t
        for d in range(1, nx):
            bx_copy(d, b).start()

    def b_three(b):
        for d in range(1, nx):
            bx_copy(d, b).wait_recv()
        t = b2[b]
        for d in range(1, nx):
            t = t + b_xr[d - 1, b]
        b3[b] = t
        gb_copy(b).start()
        dw_ref[:, cols_of(GROUPS[b], 1)] = t.reshape(nx * rx, HD)

    def b_last(b):
        gb_copy(b).wait_recv()
        dw_ref[:, cols_of(GROUPS[b], 1)] = gb[b].reshape(nx * rx, HD)

    count = len(GROUPS)

    def waves(stages, gap):
        order = []
        for w in range(count + gap * len(stages)):
            if w < nb:
                order.append((rows_of, w))
            for lag, stage in enumerate(stages):
                if 0 <= w - gap * lag < count:
                    order.append((stage, w - gap * lag))
        for work, i in order:
            work(i)

    @pl.when(c == 0)
    def _():
        waves((a_one, a_two, a_three, a_four), 1)
        for b in range(count):
            b_last(b)

    @pl.when(c == 1)
    def _():
        waves((b_one, b_two, b_three), 1)
        for a in range(count):
            a_last(a)

    for i in range(nb):
        out_copy(i).wait()

    def drain_state(p, carry):
        @pl.when(z < nz - 1)
        def _():
            remote(kst.at[1, p], kst.at[0, p], zk_s.at[p], zk_r.at[p], at(z_=z)).wait_send()

        @pl.when(z > 0)
        def _():
            remote(qst.at[1, p], qst.at[0, p], zq_s.at[p], zq_r.at[p], at(z_=z)).wait_send()

        for d in range(1, ny):
            remote(kst.at[0, p], kyr.at[d - 1, p], yk_s.at[d - 1, p], yk_r.at[d - 1, p], at(y_=ypeer(d))).wait_send()
            remote(qst.at[0, p], qyr.at[d - 1, p], yq_s.at[d - 1, p], yq_r.at[d - 1, p], at(y_=ypeer(d))).wait_send()
        return carry

    lax.fori_loop(0, H, drain_state, 0)
    for j in range(3):
        core_copy(0, j).wait_send()
        core_copy(1, j).wait_send()

    @pl.when(c == 0)
    def _():
        for a in range(count):
            for d in range(1, nx):
                ax_copy(d, a).wait_send()
                ag_copy(d, a).wait_send()
            for d in range(1, ny):
                ay_copy(d, a).wait_send()
            for d in range(1, nz):
                az_copy(d, a).wait_send()
            for d in range(nx):
                af_copy(d, a).wait_send()

    @pl.when(c == 1)
    def _():
        for b in range(count):
            for d in range(1, ny):
                by_copy(d, b).wait_send()
            for d in range(1, nz):
                bz_copy(d, b).wait_send()
            for d in range(1, nx):
                bx_copy(d, b).wait_send()
            gb_copy(b).wait_send()


BLOCKS = 4


def hand_over(dx_ref, dw_ref, dx_out, dw_out):
    dx_out[0] = dx_ref[...]
    dw_out[...] = dw_ref[...]


def shards(nz, ny, nx, inputs, weights, out_grad):
    record, cot = inputs[0], out_grad[0]
    tok, dm = record.shape
    nb = tok // CH
    rx = dm // (nz * ny * nx)
    na = ns = len(GROUPS)
    V = pltpu.VMEM
    D = pltpu.SemaphoreType.DMA
    scratch = [
        V((tok, 3 * HD), BF16),
        V((3, H, tok, HD), BF16), V((H, tok, HD), BF16),
        V((nb, H, HD, HD), F32), V((nb, H, HD, HD), F32),
        V((3, H, tok, HD), F32), V((tok, 3 * H * HD), BF16), V((dm, tok), BF16),
        V((tok, dm), BF16), D((nb,)),
        V((2, H, HD, HD), F32), V((2, H, HD, HD), F32),
        V((ny - 1, H, HD, HD), F32), V((ny - 1, H, HD, HD), F32),
        V((4, 3, nz, ny, nx, rx, HD), F32), V((2, 3, nz, ny, nx, rx, HD), F32),
        V((nx - 1, na, nz, ny, rx, HD), F32), V((ny - 1, na, nz, rx, HD), F32),
        V((na, nz, rx, HD), F32), V((nz - 1, na, rx, HD), F32), V((2, nx, na, rx, HD), F32),
        V((ny - 1, ns, nz, nx, rx, HD), F32), V((nz - 1, ns, nx, rx, HD), F32),
        V((ns, nx, rx, HD), F32), V((nx - 1, ns, nx, rx, HD), F32),
        V((ns, nx, rx, HD), F32), V((ns, nx, rx, HD), F32),
        D((H,)), D((H,)), D((H,)), D((H,)),
        D((ny - 1, H)), D((ny - 1, H)), D((ny - 1, H)), D((ny - 1, H)),
        D((2, 3)), D((2, 3)), D((nx - 1, na)), D((nx - 1, na)), D((ny - 1, na)), D((ny - 1, na)),
        D((nz - 1, na)), D((nz - 1, na)), D((nx - 1, na)), D((nx - 1, na)), D((nx, na)), D((nx, na)),
        D((ny - 1, ns)), D((ny - 1, ns)), D((nz - 1, ns)), D((nz - 1, ns)),
        D((nx - 1, ns)), D((nx - 1, ns)), D((ns,)), D((ns,)),
    ]
    vm = pl.BlockSpec(memory_space=pltpu.VMEM)
    hbm = pl.BlockSpec(memory_space=pl.ANY)
    dx, dw = pl.pallas_call(
        functools.partial(kernel, (nz, ny, nx)),
        out_shape=(
            jax.ShapeDtypeStruct((tok, dm), BF16),
            jax.ShapeDtypeStruct((dm // (nz * ny), weights.shape[1]), F32),
        ),
        in_specs=[vm, vm, vm],
        out_specs=(hbm, vm),
        scratch_shapes=scratch,
        compiler_params=pltpu.CompilerParams(
            collective_id=0, has_side_effects=True, vmem_limit_bytes=60 * 1024 * 1024
        ),
    )(record, weights, cot)
    m, k, wide = tok // BLOCKS, dw.shape[0] // BLOCKS, dw.shape[1]
    return pl.pallas_call(
        hand_over,
        grid=(BLOCKS,),
        out_shape=(jax.ShapeDtypeStruct((1, tok, dm), BF16), jax.ShapeDtypeStruct(dw.shape, F32)),
        in_specs=[pl.BlockSpec((m, dm), lambda i: (i, 0)), pl.BlockSpec((k, wide), lambda i: (i, 0))],
        out_specs=(pl.BlockSpec((1, m, dm), lambda i: (0, i, 0)), pl.BlockSpec((k, wide), lambda i: (i, 0))),
    )(dx, dw)


def solution(mesh):
    nx = mesh.shape["dp"] // 2
    ny = nx if mesh.shape["tm"] % nx == 0 else 1
    nz = mesh.shape["tm"] // ny
    return jax.shard_map(
        functools.partial(shards, nz, ny, nx),
        mesh=mesh,
        in_specs=(P("dp", "tm", None), P(), P("dp", "tm", None)),
        out_specs=(P("dp", "tm", None), P("tm", None)),
        check_vma=False,
    )
```

```python
import functools

import jax
import jax.numpy as jnp
from jax import lax
from jax.experimental import pallas as pl
from jax.experimental.pallas import tpu as pltpu
from jax.sharding import PartitionSpec as P

H = 4
HD = 128
CH = 256
MESH = pl.DeviceIdType.MESH
F32 = jnp.float32
BF16 = jnp.bfloat16
NN = (((1,), (0,)), ((), ()))
NT = (((1,), (1,)), ((), ()))
TN = (((0,), (0,)), ((), ()))


def mm(a, b, dims=NN):
    return lax.dot_general(a, b, dims, preferred_element_type=F32)


GROUPS = tuple((slot, j) for slot in range(2) for j in range(3))


def kernel(
    sizes,
    x_hbm, w_ref, og_hbm, dx_ref, dw_ref,
    x_ref, og_ref, in_sem, dcat, qkv, sc, kvg, qgg, loc, dqkv, xt, dxs, dx_sem,
    kst, qst, kyr, qyr,
    part, crecv, a_xr, a_yr, a2, a_zr, ga, b_yr, b_zr, b2, b_xr, b3, gb,
    zk_s, zk_r, zq_s, zq_r, yk_s, yk_r, yq_s, yq_r,
    c_s, c_r, ax_s, ax_r, ay_s, ay_r, az_s, az_r, ag_s, ag_r, af_s, af_r,
    by_s, by_r, bz_s, bz_r, bx_s, bx_r, gb_s, gb_r,
):
    nz, ny, nx = sizes
    tok = x_ref.shape[0]
    nb = tok // CH
    width = H * HD
    rx = dw_ref.shape[0] // nx
    dm = x_ref.shape[1]
    tm, dp = lax.axis_index("tm"), lax.axis_index("dp")
    z, y = tm // ny, lax.rem(tm, ny)
    x, c = dp // 2, lax.rem(dp, 2)

    def at(z_=None, y_=None, x_=None, c_=None):
        z_ = z if z_ is None else z_
        y_ = y if y_ is None else y_
        x_ = x if x_ is None else x_
        c_ = c if c_ is None else c_
        return (z_ * ny + y_, x_ * 2 + c_)

    def zpeer(d):
        return lax.rem(z + d, nz)

    def ypeer(d):
        return lax.rem(y + d, ny)

    def xpeer(d):
        return lax.rem(x + d, nx)

    def remote(src, dst, send, recv, device):
        return pltpu.make_async_remote_copy(
            src_ref=src, dst_ref=dst, send_sem=send, recv_sem=recv,
            device_id=device, device_id_type=MESH,
        )

    def head(p):
        return 2 * lax.rem(p + 1 - c, 2) + p // 2

    peers = [at(c_=1 - c)]
    for d in range(1, nx):
        peers += [at(x_=xpeer(d))]
    peers += [at(y_=ypeer(d)) for d in range(1, ny)]
    peers += [at(z_=zpeer(d)) for d in range(1, nz)]
    barrier = pltpu.get_barrier_semaphore()
    for peer in peers:
        pl.semaphore_signal(barrier, inc=1, device_id=peer, device_id_type=MESH)

    def block_copies(n):
        rows = pl.ds(pl.multiple_of(n * CH, CH), CH)
        return (
            pltpu.make_async_copy(x_hbm.at[rows, :], x_ref.at[rows, :], in_sem.at[0, n]),
            pltpu.make_async_copy(og_hbm.at[rows, :], og_ref.at[rows, :], in_sem.at[1, n]),
        )

    for n in range(nb):
        for copy in block_copies(n):
            copy.start()

    def project(n, carry):
        rows = pl.ds(pl.multiple_of(n * CH, CH), CH)
        for copy in block_copies(n):
            copy.wait()
        r = mm(x_ref[rows, :], w_ref[...]).astype(BF16)
        pos = tm * tok + n * CH + lax.broadcasted_iota(jnp.int32, (CH, 1), 0)
        factor = 1.0 / jnp.sqrt(jnp.float32(HD) * (pos.astype(F32) + 1.0))
        g = (og_ref[rows, :].astype(F32) * factor).astype(BF16)
        for h in range(H):
            q = r[:, h * HD : (h + 1) * HD]
            k = r[:, width + h * HD : width + (h + 1) * HD]
            v = r[:, 2 * width + h * HD : 2 * width + (h + 1) * HD]
            s = g[:, h * HD : (h + 1) * HD]
            qkv[0, h, rows, :] = q
            qkv[1, h, rows, :] = k
            qkv[2, h, rows, :] = v
            sc[h, rows, :] = s
            kvg[n, h] = mm(k, v, TN)
            qgg[n, h] = mm(q, s, TN)
        return carry

    lax.fori_loop(0, nb, project, 0)

    pl.semaphore_wait(barrier, len(peers))

    @pl.when(z == 0)
    def _():
        kst[0] = jnp.zeros_like(kst[0])

    @pl.when(z == nz - 1)
    def _():
        qst[0] = jnp.zeros_like(qst[0])

    def link(p, ord_, last, nxt, st, grp, zs, zr, ys, yr_, ybuf, later):
        @pl.when(ord_ > 0)
        def _():
            remote(st.at[1, p], st.at[0, p], zs.at[p], zr.at[p], at(z_=z)).wait_recv()

        hh = head(p)
        total = st[0, p]
        for n in range(nb):
            total = total + grp[n, hh]
        st[1, p] = total

        @pl.when(ord_ < nz - 1)
        def _():
            remote(st.at[1, p], st.at[0, p], zs.at[p], zr.at[p], at(z_=nxt)).start()

        for d in range(1, ny):
            other = ypeer(d)
            which = jnp.where(later(other), 1, 0)
            remote(
                st.at[which, p], ybuf.at[d - 1, p], ys.at[d - 1, p], yr_.at[d - 1, p],
                at(y_=other),
            ).start()

    def local(n, p):
        hh = head(p)
        rows = pl.ds(pl.multiple_of(n * CH, CH), CH)
        q, k, v, s = qkv[0, hh, rows, :], qkv[1, hh, rows, :], qkv[2, hh, rows, :], sc[hh, rows, :]
        row = lax.broadcasted_iota(jnp.int32, (CH, CH), 0)
        col = lax.broadcasted_iota(jnp.int32, (CH, CH), 1)
        low, up = row >= col, row <= col
        vg = jnp.where(low, mm(s, v, NT), 0.0).astype(BF16)
        vgt = jnp.where(up, mm(v, s, NT), 0.0).astype(BF16)
        qkt = jnp.where(up, mm(k, q, NT), 0.0).astype(BF16)
        loc[0, p, rows, :] = mm(vg, k)
        loc[1, p, rows, :] = mm(vgt, q)
        loc[2, p, rows, :] = mm(qkt, s)

    def core_copy(slot, j):
        return remote(part.at[2 * slot, j], crecv.at[slot, j], c_s.at[slot, j], c_r.at[slot, j], at(c_=1 - c))

    def mine(g):
        return part.at[2 * g[0] + 1, g[1]]

    def ax_copy(d, a):
        o = xpeer(d)
        return remote(
            mine(GROUPS[a]).at[:, :, o], a_xr.at[d - 1, a], ax_s.at[d - 1, a], ax_r.at[d - 1, a], at(x_=o)
        )

    def ay_copy(d, a):
        o = ypeer(d)
        return remote(
            mine(GROUPS[a]).at[:, o, x], a_yr.at[d - 1, a], ay_s.at[d - 1, a], ay_r.at[d - 1, a], at(y_=o)
        )

    def az_copy(d, a):
        o = zpeer(d)
        return remote(a2.at[a, o], a_zr.at[d - 1, a], az_s.at[d - 1, a], az_r.at[d - 1, a], at(z_=o))

    def by_copy(d, b):
        o = ypeer(d)
        return remote(
            mine(GROUPS[b]).at[:, o], b_yr.at[d - 1, b], by_s.at[d - 1, b], by_r.at[d - 1, b], at(y_=o)
        )

    def bz_copy(d, b):
        o = zpeer(d)
        return remote(
            mine(GROUPS[b]).at[o, y], b_zr.at[d - 1, b], bz_s.at[d - 1, b], bz_r.at[d - 1, b], at(z_=o)
        )

    def bx_copy(d, b):
        o = xpeer(d)
        return remote(b2.at[b], b_xr.at[d - 1, b], bx_s.at[d - 1, b], bx_r.at[d - 1, b], at(x_=o))

    def gb_copy(b):
        return remote(b3.at[b], gb.at[b], gb_s.at[b], gb_r.at[b], at(c_=1 - c))

    def ag_copy(d, a):
        return remote(
            ga.at[0, 0, a], ga.at[0, d, a], ag_s.at[d - 1, a], ag_r.at[d - 1, a], at(x_=xpeer(d))
        )

    def af_copy(d, a):
        return remote(ga.at[0, d, a], ga.at[1, d, a], af_s.at[d, a], af_r.at[d, a], at(c_=1 - c))

    def finish(p):
        hh = head(p)
        start, end = kst[0, p], qst[0, p]
        for d in range(1, ny):
            remote(kst.at[0, p], kyr.at[d - 1, p], yk_s.at[d - 1, p], yk_r.at[d - 1, p], at(y_=ypeer(d))).wait_recv()
            remote(qst.at[0, p], qyr.at[d - 1, p], yq_s.at[d - 1, p], yq_r.at[d - 1, p], at(y_=ypeer(d))).wait_recv()
            start = start + kyr[d - 1, p]
            end = end + qyr[d - 1, p]
        cols = [pl.ds(pl.multiple_of(j * width + hh * HD, HD), HD) for j in range(3)]
        for n in range(nb):
            rows = pl.ds(n * CH, CH)
            dq = loc[0, p, rows, :] + mm(sc[hh, rows, :], start.astype(BF16), NT)
            dqkv[rows, cols[0]] = dq.astype(BF16)
            dcat[rows, :HD] = dq.astype(BF16)
            start = start + kvg[n, hh]
        for n in range(nb - 1, -1, -1):
            rows = pl.ds(n * CH, CH)
            after = end.astype(BF16)
            dk = loc[1, p, rows, :] + mm(qkv[2, hh, rows, :], after, NT)
            dv = loc[2, p, rows, :] + mm(qkv[1, hh, rows, :], after)
            dqkv[rows, cols[1]] = dk.astype(BF16)
            dqkv[rows, cols[2]] = dv.astype(BF16)
            dcat[rows, HD : 2 * HD] = dk.astype(BF16)
            dcat[rows, 2 * HD :] = dv.astype(BF16)
            end = end + qgg[n, hh]
        zb = 2 if nz % 2 == 0 else 1
        m = zb * (dm // nz)

        def slab(i, carry):
            rows = pl.ds(pl.multiple_of(i * m, m), m)
            r = mm(xt[rows, :], dcat[...])
            for j in range(3):
                part[p, j, pl.ds(i * zb, zb)] = r[:, j * HD : (j + 1) * HD].reshape(zb, ny, nx, rx, HD)
            return carry

        lax.fori_loop(0, nz // zb, slab, 0)

    def head_step(p):
        finish(p)
        slot = p // 2

        @pl.when(lax.rem(p, 2) == 0)
        def _():
            for j in range(3):
                core_copy(slot, j).start()

        @pl.when(lax.rem(p, 2) == 1)
        def _():
            for j in range(3):
                core_copy(slot, j).wait_recv()
                for i in range(nz):
                    part[p, j, i] = part[p, j, i] + crecv[slot, j, i]
                for s_ in range(2):

                    @pl.when((slot == s_) & (c == 0))
                    def _():
                        for d in range(1, nx):
                            ax_copy(d, GROUPS.index((s_, j))).start()

                    @pl.when((slot == s_) & (c == 1))
                    def _():
                        for d in range(1, ny):
                            by_copy(d, GROUPS.index((s_, j))).start()

    items = nb * (H + 1)
    per = 1
    while any((nz + p + 1) * per < nb * (p + 2) for p in range(H)):
        per += 1

    def step(i, carry):
        kp = i - z
        qp = i - (nz - 1 - z)

        @pl.when((kp >= 0) & (kp < H))
        def _():
            link(kp, z, nz, z + 1, kst, kvg, zk_s, zk_r, yk_s, yk_r, kyr, lambda o: o > y)

        @pl.when((qp >= 0) & (qp < H))
        def _():
            link(qp, nz - 1 - z, nz, z - 1, qst, qgg, zq_s, zq_r, yq_s, yq_r, qyr, lambda o: o < y)

        def piece(u, carry):
            idx = i * per + u
            group, n = idx // nb, lax.rem(idx, nb)

            @pl.when((idx < items) & (group != 1))
            def _():
                local(n, jnp.where(group == 0, 0, group - 1))

            @pl.when(group == 1)
            def _():
                rows = pl.ds(pl.multiple_of(n * CH, CH), CH)
                xt[:, rows] = x_ref[rows, :].T

            return carry

        lax.fori_loop(0, per, piece, 0)

        @pl.when(i >= nz)
        def _():
            head_step(i - nz)

        return carry

    lax.fori_loop(0, nz + H, step, 0)

    def out_copy(i):
        rows = pl.ds(i * CH, CH)
        return pltpu.make_async_copy(dxs.at[rows, :], dx_ref.at[rows, :], dx_sem.at[i])

    def rows_of(i):
        rows = pl.ds(i * CH, CH)
        dxs[rows, :] = mm(dqkv[rows, :], w_ref[...], NT).astype(BF16)
        out_copy(i).start()

    def a_one(a):
        for d in range(1, nx):
            ax_copy(d, a).wait_recv()
        own = mine(GROUPS[a])
        for i in range(nz):
            t = own[i, :, x]
            for d in range(1, nx):
                t = t + a_xr[d - 1, a, i]
            own[i, :, x] = t
        for d in range(1, ny):
            ay_copy(d, a).start()

    def a_two(a):
        for d in range(1, ny):
            ay_copy(d, a).wait_recv()
        own = mine(GROUPS[a])
        for i in range(nz):
            t = own[i, y, x]
            for d in range(1, ny):
                t = t + a_yr[d - 1, a, i]
            a2[a, i] = t
        for d in range(1, nz):
            az_copy(d, a).start()

    def a_three(a):
        for d in range(1, nz):
            az_copy(d, a).wait_recv()
        t = a2[a, z]
        for d in range(1, nz):
            t = t + a_zr[d - 1, a]
        ga[0, 0, a] = t
        for d in range(1, nx):
            ag_copy(d, a).start()
        af_copy(0, a).start()

    def cols_of(g, core):
        return pl.ds(pl.multiple_of(g[1] * width + (2 * core + g[0]) * HD, HD), HD)

    def place(flip, d, a):
        rows = pl.ds(pl.multiple_of(lax.rem(x - d + nx, nx) * rx, rx), rx)
        dw_ref[rows, cols_of(GROUPS[a], 0)] = ga[flip, d, a]

    def a_four(a):
        for d in range(1, nx):
            ag_copy(d, a).wait_recv()
            af_copy(d, a).start()
        for d in range(nx):
            place(0, d, a)

    def a_last(a):
        for d in range(nx):
            af_copy(d, a).wait_recv()
            place(1, d, a)

    def b_one(b):
        for d in range(1, ny):
            by_copy(d, b).wait_recv()
        own = mine(GROUPS[b])
        for i in range(nz):
            t = own[i, y]
            for d in range(1, ny):
                t = t + b_yr[d - 1, b, i]
            own[i, y] = t
        for d in range(1, nz):
            bz_copy(d, b).start()

    def b_two(b):
        for d in range(1, nz):
            bz_copy(d, b).wait_recv()
        t = mine(GROUPS[b])[z, y]
        for d in range(1, nz):
            t = t + b_zr[d - 1, b]
        b2[b] = t
        for d in range(1, nx):
            bx_copy(d, b).start()

    def b_three(b):
        for d in range(1, nx):
            bx_copy(d, b).wait_recv()
        t = b2[b]
        for d in range(1, nx):
            t = t + b_xr[d - 1, b]
        b3[b] = t
        gb_copy(b).start()
        dw_ref[:, cols_of(GROUPS[b], 1)] = t.reshape(nx * rx, HD)

    def b_last(b):
        gb_copy(b).wait_recv()
        dw_ref[:, cols_of(GROUPS[b], 1)] = gb[b].reshape(nx * rx, HD)

    count = len(GROUPS)

    def waves(stages, gap):
        order = []
        for w in range(count + gap * len(stages)):
            if w < nb:
                order.append((rows_of, w))
            for lag, stage in enumerate(stages):
                if 0 <= w - gap * lag < count:
                    order.append((stage, w - gap * lag))
        for work, i in order:
            work(i)

    @pl.when(c == 0)
    def _():
        waves((a_one, a_two, a_three, a_four), 1)
        for b in range(count):
            b_last(b)

    @pl.when(c == 1)
    def _():
        waves((b_one, b_two, b_three), 1)
        for a in range(count):
            a_last(a)

    for i in range(nb):
        out_copy(i).wait()

    def drain_state(p, carry):
        @pl.when(z < nz - 1)
        def _():
            remote(kst.at[1, p], kst.at[0, p], zk_s.at[p], zk_r.at[p], at(z_=z)).wait_send()

        @pl.when(z > 0)
        def _():
            remote(qst.at[1, p], qst.at[0, p], zq_s.at[p], zq_r.at[p], at(z_=z)).wait_send()

        for d in range(1, ny):
            remote(kst.at[0, p], kyr.at[d - 1, p], yk_s.at[d - 1, p], yk_r.at[d - 1, p], at(y_=ypeer(d))).wait_send()
            remote(qst.at[0, p], qyr.at[d - 1, p], yq_s.at[d - 1, p], yq_r.at[d - 1, p], at(y_=ypeer(d))).wait_send()
        return carry

    lax.fori_loop(0, H, drain_state, 0)
    for j in range(3):
        core_copy(0, j).wait_send()
        core_copy(1, j).wait_send()

    @pl.when(c == 0)
    def _():
        for a in range(count):
            for d in range(1, nx):
                ax_copy(d, a).wait_send()
                ag_copy(d, a).wait_send()
            for d in range(1, ny):
                ay_copy(d, a).wait_send()
            for d in range(1, nz):
                az_copy(d, a).wait_send()
            for d in range(nx):
                af_copy(d, a).wait_send()

    @pl.when(c == 1)
    def _():
        for b in range(count):
            for d in range(1, ny):
                by_copy(d, b).wait_send()
            for d in range(1, nz):
                bz_copy(d, b).wait_send()
            for d in range(1, nx):
                bx_copy(d, b).wait_send()
            gb_copy(b).wait_send()


def shards(nz, ny, nx, inputs, weights, out_grad):
    record, cot = inputs[0], out_grad[0]
    tok, dm = record.shape
    nb = tok // CH
    rx = dm // (nz * ny * nx)
    na = ns = len(GROUPS)
    V = pltpu.VMEM
    D = pltpu.SemaphoreType.DMA
    scratch = [
        V((tok, dm), BF16), V(cot.shape, BF16), D((2, nb)), V((tok, 3 * HD), BF16),
        V((3, H, tok, HD), BF16), V((H, tok, HD), BF16),
        V((nb, H, HD, HD), F32), V((nb, H, HD, HD), F32),
        V((3, H, tok, HD), F32), V((tok, 3 * H * HD), BF16), V((dm, tok), BF16),
        V((tok, dm), BF16), D((nb,)),
        V((2, H, HD, HD), F32), V((2, H, HD, HD), F32),
        V((ny - 1, H, HD, HD), F32), V((ny - 1, H, HD, HD), F32),
        V((4, 3, nz, ny, nx, rx, HD), F32), V((2, 3, nz, ny, nx, rx, HD), F32),
        V((nx - 1, na, nz, ny, rx, HD), F32), V((ny - 1, na, nz, rx, HD), F32),
        V((na, nz, rx, HD), F32), V((nz - 1, na, rx, HD), F32), V((2, nx, na, rx, HD), F32),
        V((ny - 1, ns, nz, nx, rx, HD), F32), V((nz - 1, ns, nx, rx, HD), F32),
        V((ns, nx, rx, HD), F32), V((nx - 1, ns, nx, rx, HD), F32),
        V((ns, nx, rx, HD), F32), V((ns, nx, rx, HD), F32),
        D((H,)), D((H,)), D((H,)), D((H,)),
        D((ny - 1, H)), D((ny - 1, H)), D((ny - 1, H)), D((ny - 1, H)),
        D((2, 3)), D((2, 3)), D((nx - 1, na)), D((nx - 1, na)), D((ny - 1, na)), D((ny - 1, na)),
        D((nz - 1, na)), D((nz - 1, na)), D((nx - 1, na)), D((nx - 1, na)), D((nx, na)), D((nx, na)),
        D((ny - 1, ns)), D((ny - 1, ns)), D((nz - 1, ns)), D((nz - 1, ns)),
        D((nx - 1, ns)), D((nx - 1, ns)), D((ns,)), D((ns,)),
    ]
    vm = pl.BlockSpec(memory_space=pltpu.VMEM)
    hbm = pl.BlockSpec(memory_space=pl.ANY)
    dx, dw = pl.pallas_call(
        functools.partial(kernel, (nz, ny, nx)),
        out_shape=(
            jax.ShapeDtypeStruct((tok, dm), BF16),
            jax.ShapeDtypeStruct((dm // (nz * ny), weights.shape[1]), F32),
        ),
        in_specs=[hbm, vm, hbm],
        out_specs=(hbm, vm),
        scratch_shapes=scratch,
        compiler_params=pltpu.CompilerParams(
            collective_id=0, has_side_effects=True, vmem_limit_bytes=60 * 1024 * 1024
        ),
    )(record, weights, cot)
    return dx[None], dw


def solution(mesh):
    nx = mesh.shape["dp"] // 2
    ny = nx if mesh.shape["tm"] % nx == 0 else 1
    nz = mesh.shape["tm"] // ny
    return jax.shard_map(
        functools.partial(shards, nz, ny, nx),
        mesh=mesh,
        in_specs=(P("dp", "tm", None), P(), P("dp", "tm", None)),
        out_specs=(P("dp", "tm", None), P("tm", None)),
        check_vma=False,
    )
```
